128 devices in a mesh: ctx: 16 (over z_hi, x, core), head: 8 (over z_lo, y).
Axes of the slice: x: 4, y: 4, z: 4 (z_hi: 2, z_lo: 2; z = z_hi * 2 + z_lo), core: 2. Of those that a mesh axis runs over, the one named last changes fastest.
Arguments:
- tokens: bfloat16 [16384, 4096], P('ctx', 'head'), may hold values from -23 to 23
- proj_weight: bfloat16 [4096, 32, 384], P(None, 'head'), may hold values from -1 to 1
- partner_shard: int32 [32, 256, 3], P('head'), may hold values from 0 to 15, all different within a row; in each aligned block of 16 rows (0 to 15, 16 to 31, ..., all dimensions but the last counted through in order) at most 6 rows name the same one
- partner_block: int32 [32, 256, 3], P('head'), may hold values from 0 to 15
Outputs:
- attended: bfloat16 [16384, 32, 128], P('ctx', 'head')
The draws below stay inside these ranges and needn't reach their ends.
Inputs may be any that keep to these rules, and one draw needn't show every extreme that they name: `partner_shard`: the 3 entries of one row differ. For each head, within each aligned run of 16 block rows, no value is named more than 6 times, and some runs name one value exactly 6 times.
All inputs are finite; a program needn't handle non-finite values.
Results may differ from the reference program's by a relative error of at most 0.008.
Values may be sent and summed in bfloat16 or wider, within the bound.
A program may use at most 192 MiB of HBM per device.

```python
import math
import jax
import jax.numpy as jnp
import numpy as np
from jax import lax

D = 4096
NH = 32
HEAD_DIMENSION = 128
BLK = 64
GLOB = 2
RAND = 3
BPD = 16
SEQUENCE_TOKENS = 16384
NB = 256
MOST = 6
N_CTX = 16


def draw_tokens(key, part):
    key_base = jax.random.fold_in(jax.random.fold_in(key, 11), 0)
    values = jax.random.truncated_normal(key_base, -4.0, 4.0, (SEQUENCE_TOKENS, D), jnp.float32)
    return values.astype(jnp.bfloat16)


def draw_proj_weight(key, part):
    values = jax.random.truncated_normal(jax.random.fold_in(key, 23), -4.0, 4.0, (D, NH, 3 * HEAD_DIMENSION), jnp.float32) * D ** (-0.5)
    return values.astype(jnp.bfloat16)


def plant(drawn, stream_key, least, high):
    place = [jax.random.randint(jax.random.fold_in(stream_key, axis), (), 0, length) for axis, length in enumerate(drawn.shape)]
    main_axis = drawn.shape.index(max(drawn.shape))
    beside = place[:main_axis] + [(place[main_axis] + 1) % drawn.shape[main_axis]] + place[main_axis + 1:]
    return drawn.at[tuple(place)].set(least).at[tuple(beside)].set(high)


def routed_block(rng, own, number, rows, number_of, top, most, lean):
    order = jax.random.permutation(rng, number_of)
    heavy_load, usual = portions_of(number_of, rows * top, most, lean, True), portions_of(number_of, rows * top, most, lean, False)
    places = jnp.arange(number_of)

    def named(tallies, rotation):
        used = int((tallies > 0).sum())
        fixed = max(1, used // 4)
        shifted = fixed + (places - fixed + rotation * (used - fixed)) % max(1, number_of - fixed)
        return jnp.zeros((number_of,), jnp.int32).at[order[jnp.where(places < fixed, places, shifted)]].set(jnp.asarray(tallies, jnp.int32))

    tallies = jnp.where(number % 4 == 0, named(heavy_load, number // 4), named(usual, number - number // 4 - 1))
    mixed = jax.random.permutation(jax.random.fold_in(own, 3), number_of)
    giver, taker = mixed[0:number_of // 2 * 2:2], mixed[1:number_of // 2 * 2:2]
    slack = jnp.minimum(tallies[giver] - 1, most - tallies[taker]) // 2
    slack = jnp.where((giver == order[0]) | (taker == order[0]) | (tallies[taker] == 0), 0, jnp.maximum(slack, 0))
    shifted = jax.random.randint(jax.random.fold_in(own, 4), (number_of // 2,), 0, 1 << 20) % (slack + 1)
    tallies = tallies.at[giver].add(-shifted).at[taker].add(shifted)
    items = jnp.searchsorted(jnp.cumsum(tallies), jnp.arange(rows * top), side="right").astype(jnp.int32)
    table = items.reshape(top, rows).T
    table = table[jax.random.permutation(jax.random.fold_in(own, 1), rows)]
    rotation = jax.random.randint(jax.random.fold_in(own, 2), (rows, 1), 0, top)
    return jnp.take_along_axis(table, (jnp.arange(top)[None, :] + rotation) % top, axis=1)


def portions_of(number_of, total, most, slope, full):
    portions = [(1 << 20) // math.isqrt(standing ** slope) + 1 for standing in range(1, number_of + 1)]
    largest = most if full else min(most, max(-(-total // number_of), total * portions[0] // sum(portions)))
    least = 1 if total - largest >= number_of - 1 else 0
    holding, rest = [largest] + [least] * (number_of - 1), total - largest - least * (number_of - 1)
    while rest > 0:
        candidates = [i for i in range(1, number_of) if holding[i] < largest] or [i for i in range(1, number_of) if holding[i] < most]
        mass, budget = sum([portions[i] for i in candidates]), rest
        for i in candidates:
            extra = min(most - holding[i], max(1, budget * portions[i] // mass), rest)
            holding[i] = holding[i] + extra
            rest = rest - extra
    return np.array(holding)


def setup_inputs(seed: int = 0) -> dict:
    arg_keys = jax.random.split(jax.random.key(seed), 5)
    tokens = draw_tokens(jax.random.fold_in(arg_keys[4], 71), 0)
    proj_weight = draw_proj_weight(jax.random.fold_in(arg_keys[4], 71), 0)
    partner_shard_keys = jax.random.split(jax.random.fold_in(arg_keys[2], 1), NH * NB // BPD)
    partner_shard_turns = jax.random.permutation(jax.random.fold_in(arg_keys[2], 3), NH * NB // BPD)
    partner_shard = jax.vmap(lambda own, number: routed_block(jax.random.fold_in(arg_keys[2], 2), own, number, BPD, N_CTX, RAND, MOST, 2))(partner_shard_keys, partner_shard_turns).reshape((NH, NB, RAND))
    partner_block = plant(jax.random.randint(arg_keys[3], (NH, NB, RAND), 0, BPD), jax.random.fold_in(arg_keys[3], 1), 0, BPD - 1).astype(jnp.int32)
    return {"tokens": tokens, "proj_weight": proj_weight, "partner_shard": partner_shard, "partner_block": partner_block}


def reference(tokens, proj_weight, partner_shard, partner_block):
    flat_weight = proj_weight.reshape(D, NH * 3 * HEAD_DIMENSION)
    packed = jnp.dot(tokens, flat_weight, preferred_element_type=jnp.float32).astype(jnp.bfloat16)
    packed = jnp.transpose(packed.reshape(SEQUENCE_TOKENS, NH, 3 * HEAD_DIMENSION), (1, 0, 2))
    partner = (partner_shard * BPD + partner_block).astype(jnp.int32)
    inverse_root_scale = HEAD_DIMENSION ** -0.5

    def one_head(inputs):
        head_pack, indices = inputs
        head_pack = head_pack.astype(jnp.float32)
        queries = head_pack[:, :HEAD_DIMENSION]
        keys = head_pack[:, HEAD_DIMENSION:2 * HEAD_DIMENSION]
        values = head_pack[:, 2 * HEAD_DIMENSION:]
        blocked_query_rows = queries.reshape(NB, BLK, HEAD_DIMENSION)

        def gather_set(field):
            field_blocks = field.reshape(NB, BLK, HEAD_DIMENSION)
            leading = jnp.broadcast_to(field_blocks[:GLOB].reshape(1, GLOB * BLK, HEAD_DIMENSION), (NB, GLOB * BLK, HEAD_DIMENSION))
            partners = field_blocks[indices].reshape(NB, RAND * BLK, HEAD_DIMENSION)
            return jnp.concatenate([jnp.roll(field_blocks, 1, 0), field_blocks, jnp.roll(field_blocks, -1, 0), leading, partners], axis=1)

        partner_key_rows = gather_set(keys)
        partner_value_rows = gather_set(values)
        logit_scores = jnp.einsum("msx,mix->msi", blocked_query_rows, partner_key_rows, precision=lax.Precision.HIGHEST) * inverse_root_scale
        softmax_weight_matrix = jax.nn.softmax(logit_scores, axis=-1).astype(jnp.bfloat16)
        softmax_weight_matrix = lax.optimization_barrier(softmax_weight_matrix).astype(jnp.float32)
        sparse_attention_output = jnp.einsum("thw,twp->thp", softmax_weight_matrix, partner_value_rows, precision=lax.Precision.HIGHEST).reshape(SEQUENCE_TOKENS, HEAD_DIMENSION)
        global_scores = jnp.dot(queries[:GLOB * BLK], keys.T, precision=lax.Precision.HIGHEST) * inverse_root_scale
        global_weights = jax.nn.softmax(global_scores, axis=-1)
        global_out = jnp.dot(global_weights, values, precision=lax.Precision.HIGHEST)
        context = jnp.concatenate([global_out, sparse_attention_output[GLOB * BLK:]], axis=0)
        return context.astype(jnp.bfloat16)

    result = lax.map(one_head, (packed, partner))
    return jnp.transpose(result, (1, 0, 2))
```

```python
import functools

import jax
import jax.numpy as jnp
from jax import lax
from jax.experimental import pallas as pl
from jax.experimental.pallas import tpu as pltpu
from jax.sharding import PartitionSpec as P

HD = 128
BLK = 64
ROWS = 1024
D = 4096
FEAT = 512
MESH = pl.DeviceIdType.MESH
CHUNKS = (256, 256, 256, 128, 128)
C2 = 1.4426950408889634 * HD**-0.5


def kernel(
    tokens, weight, part_shard, part_block, out,
    tok, stage, wv, pk, kv, q, gq, gout, gm, gl, gacc, obuf, orecv,
    wsem, lsem, ssem, rsem,
):
    ctx, hd = lax.axis_index("ctx"), lax.axis_index("head")
    zh, x, core = ctx // 8, (ctx // 2) % 4, ctx % 2
    zl, y = hd // 4, hd % 4
    g = zh * 2 + core

    def at_ctx(zh_, x_, core_):
        return (zh_ * 8 + x_ * 2 + core_, hd)

    def at_head(zl_, y_):
        return (ctx, zl_ * 4 + y_)

    up, down, far = (y + 1) % 4, (y + 3) % 4, (y + 2) % 4
    xs = [(x + d) % 4 for d in (0, 1, 2, 3)]
    zpeer = at_head(1 - zl, y)
    ypeer, mpeer = at_head(zl, up), at_head(zl, down)
    cpeer = at_ctx(zh, x, 1 - core)
    hpeer = at_ctx(1 - zh, x, core)
    dpeer = at_ctx(1 - zh, x, 1 - core)
    xpeers = [None] + [at_ctx(zh, xs[d], core) for d in (1, 2, 3)]
    gc, gz, gd = zh * 2 + 1 - core, (1 - zh) * 2 + core, (1 - zh) * 2 + 1 - core

    barrier = pltpu.get_barrier_semaphore()
    everyone = [zpeer, ypeer, mpeer, cpeer, hpeer, dpeer] + xpeers[1:]
    for peer in everyone:
        pl.semaphore_signal(barrier, inc=1, device_id=peer, device_id_type=MESH)
    pl.semaphore_wait(barrier, len(everyone))

    sems = {}
    sent = []
    local = {}

    def sem_of(key):
        return sems.setdefault(key, len(sems))

    def send(key, src, dst, peer):
        i = sem_of(key)
        copy = pltpu.make_async_remote_copy(
            src_ref=src, dst_ref=dst, send_sem=ssem.at[i], recv_sem=rsem.at[i],
            device_id=peer, device_id_type=MESH,
        )
        copy.start()
        sent.append(copy)

    def arrived(key, dst):
        i = sem_of(key)
        pltpu.make_async_remote_copy(
            src_ref=dst, dst_ref=dst, send_sem=ssem.at[i], recv_sem=rsem.at[i],
            device_id=zpeer, device_id_type=MESH,
        ).wait_recv()

    def put(key, src, dst):
        copy = pltpu.make_async_copy(src, dst, lsem.at[len(local)])
        copy.start()
        local[key] = copy

    starts = [sum(CHUNKS[:c]) for c in range(len(CHUNKS))]

    def rows_of(c):
        return pl.ds(starts[c], CHUNKS[c])

    def blocks_of(c):
        return pl.ds(starts[c] // BLK, CHUNKS[c] // BLK)

    def piece(zl_, y_, c):
        return tok.at[rows_of(c), pl.ds(pl.multiple_of((zl_ * 4 + y_) * FEAT, FEAT), FEAT)]

    def mine(c):
        return tokens.at[rows_of(c), :]

    def give_z(c):
        send(("z", c), mine(c), piece(zl, y, c), zpeer)

    def give_y(c):
        send(("yu", c), mine(c), piece(zl, y, c), ypeer)
        send(("yd", c), mine(c), piece(zl, y, c), mpeer)

    def pass_z(c):
        arrived(("z", c), piece(1 - zl, y, c))
        send(("zu", c), piece(1 - zl, y, c), piece(1 - zl, y, c), ypeer)
        send(("zd", c), piece(1 - zl, y, c), piece(1 - zl, y, c), mpeer)

    def pass_y(c):
        arrived(("yu", c), piece(zl, down, c))
        send(("fu", c), piece(zl, down, c), piece(zl, down, c), ypeer)
        arrived(("zd", c), piece(1 - zl, up, c))
        send(("fd", c), piece(1 - zl, up, c), piece(1 - zl, up, c), mpeer)

    def tokens_complete(c):
        arrived(("yd", c), piece(zl, up, c))
        arrived(("zu", c), piece(1 - zl, down, c))
        arrived(("fu", c), piece(zl, far, c))
        arrived(("fd", c), piece(1 - zl, far, c))

    def weight_copy(i):
        return pltpu.make_async_copy(
            weight.at[pl.ds(i * FEAT, FEAT)], stage.at[i % 2], wsem.at[i % 2]
        )

    def relayout(i):
        weight_copy(i).wait()
        block = jnp.swapaxes(stage[i % 2], 0, 1)
        rows = pl.ds(i * FEAT, FEAT)
        for h in range(4):
            wv[0, rows, h * HD : (h + 1) * HD] = block[h, :, :HD]
            wv[1 + h // 2, rows, (h % 2) * 256 : (h % 2 + 1) * 256] = block[h, :, HD:]
        if i + 2 < 8:
            weight_copy(i + 2).start()

    def project(c):
        def one(n, carry):
            pk[n, blocks_of(c)] = (
                jnp.dot(tok[rows_of(c), :], wv[n], preferred_element_type=jnp.float32)
                .astype(jnp.bfloat16)
                .reshape(CHUNKS[c] // BLK, BLK, 512)
            )
            return carry

        lax.fori_loop(0, 3, one, 0)

    def kv_part(h, c):
        return pk.at[1 + h // 2, blocks_of(c), :, pl.ds(pl.multiple_of((h % 2) * 256, 256), 256)]

    def q_part(h, c):
        return pk.at[0, blocks_of(c), :, pl.ds(pl.multiple_of(h * HD, HD), HD)]

    def give_x(c):
        for d in (2, 1, 3):
            send(("kv", d, c), kv_part(xs[d], c), kv.at[g * 4 + x, blocks_of(c)], xpeers[d])
        put(("kv", c), kv_part(x, c), kv.at[g * 4 + x, blocks_of(c)])
        for d in (2, 1, 3):
            send(("q", d, c), q_part(xs[d], c), q.at[x, blocks_of(c)], xpeers[d])
        put(("q", c), q_part(x, c), q.at[x, blocks_of(c)])

    def group(k, c):
        return kv.at[pl.ds(k * 4, 4), blocks_of(c)]

    def pass_x(c):
        for d in (1, 2, 3):
            arrived(("kv", d, c), kv.at[g * 4 + xs[4 - d], blocks_of(c)])
        local[("kv", c)].wait()
        send(("kz", c), group(g, c), group(g, c), hpeer)
        send(("kc", c), group(g, c), group(g, c), cpeer)
        for d in (1, 2, 3):
            arrived(("q", d, c), q.at[xs[4 - d], blocks_of(c)])
        local[("q", c)].wait()

    def pass_h(c):
        arrived(("kz", c), group(gz, c))
        send(("kd", c), group(gz, c), group(gz, c), cpeer)

    def kv_complete(c):
        arrived(("kc", c), group(gc, c))
        arrived(("kd", c), group(gd, c))

    def give_gq():
        lead = q.at[0, pl.ds(0, 2)]
        put("gq", lead, gq.at[g])
        for name, peer in (("gqc", cpeer), ("gqh", hpeer), ("gqd", dpeer)):
            send(name, lead, gq.at[g], peer)

    def take_gq():
        local["gq"].wait()
        arrived("gqc", gq.at[gc])
        arrived("gqh", gq.at[gz])
        arrived("gqd", gq.at[gd])
        gm[...] = jnp.full_like(gm, -jnp.inf)
        gl[...] = jnp.zeros_like(gl)
        gacc[...] = jnp.zeros_like(gacc)

    def lead_keys(c):
        size = CHUNKS[c]
        query = gq[0, g // 2, pl.ds(pl.multiple_of((g % 2) * 32, 32), 32), :]

        def one(k, carry):
            top, total, acc = carry
            block = kv[pl.ds(k * 4, 4), blocks_of(c)].reshape(4 * size, 256)
            s = lax.dot_general(
                query, block[:, :HD], (((1,), (1,)), ((), ())), preferred_element_type=jnp.float32
            )
            higher = jnp.maximum(top, jnp.max(s, axis=1, keepdims=True))
            p = jnp.exp2((s - higher) * C2)
            shrink = jnp.exp2((top - higher) * C2)
            total = total * shrink + jnp.sum(p, axis=1, keepdims=True)
            acc = acc * shrink + jnp.dot(
                p.astype(jnp.bfloat16), block[:, HD:], preferred_element_type=jnp.float32
            )
            return higher, total, acc

        top, total, acc = lax.fori_loop(0, 4, one, (gm[...], gl[...], gacc[...]))
        gm[...], gl[...], gacc[...] = top, total, acc

    def lead_out():
        gout[g] = (gacc[...] / gl[...]).astype(jnp.bfloat16)
        for name, peer in (("goc", cpeer), ("goh", hpeer), ("god", dpeer)):
            send(name, gout.at[g], gout.at[g], peer)

    def key_block(b):
        s, r = b // 16, b % 16
        slot = ((s // 8) * 2 + s % 2) * 4 + (s // 2) % 4
        return kv[slot, r]

    def attend(xp):
        first = (zh * 8 + xp * 2 + core) * 16

        def one(r, carry):
            b = first + r
            ids = [(b + 255) % 256, b, (b + 1) % 256, 0, 1] + [
                part_shard[j, x, b] * 16 + part_block[j, x, b] for j in range(3)
            ]
            keys = jnp.concatenate([key_block(i) for i in ids], axis=0)
            rows = pl.ds(pl.multiple_of(r * BLK, BLK), BLK)
            s = lax.dot_general(
                q[xp, r], keys[:, :HD], (((1,), (1,)), ((), ())),
                preferred_element_type=jnp.float32,
            )
            p = jnp.exp2((s - jnp.max(s, axis=1, keepdims=True)) * C2)
            total = jnp.sum(p, axis=1, keepdims=True)
            o = jnp.dot(p.astype(jnp.bfloat16), keys[:, HD:], preferred_element_type=jnp.float32)
            obuf[xp, rows, :] = (o / total).astype(jnp.bfloat16)
            return carry

        lax.fori_loop(0, 16, one, 0, unroll=2)

    last = len(CHUNKS) - 1
    weight_copy(0).start()
    weight_copy(1).start()
    give_z(0)
    give_y(0)
    give_z(1)
    put("tok", tokens, tok.at[:, pl.ds(pl.multiple_of(hd * FEAT, FEAT), FEAT)])
    for i in range(5):
        relayout(i)
    pass_z(0)
    for i in range(5, 8):
        relayout(i)
    local["tok"].wait()
    for c in range(last + 1):
        pass_y(c)
        if c + 2 <= last:
            give_z(c + 2)
        if c + 1 <= last:
            give_y(c + 1)
            pass_z(c + 1)
        if c >= 1:
            pass_x(c - 1)
            if c == 1:
                give_gq()
        if c >= 2:
            pass_h(c - 2)
        tokens_complete(c)
        project(c)
        give_x(c)
        if c >= 2:
            kv_complete(c - 2)
            if c == 2:
                take_gq()
            lead_keys(c - 2)
    pass_h(last - 1)
    pass_x(last)
    kv_complete(last - 1)
    lead_keys(last - 1)
    pass_h(last)
    kv_complete(last)
    lead_keys(last)
    lead_out()
    for d in (2, 1, 3, 0):
        attend(xs[d])
        if d == 2:
            arrived("goc", gout.at[gc])
            arrived("goh", gout.at[gz])
            arrived("god", gout.at[gd])

        @pl.when((xs[d] == 0) & (g == 0))
        def _():
            obuf[xs[d], pl.ds(0, 128), :] = gout[...].reshape(128, HD)

        if d:
            send(("o", d), obuf.at[xs[d]], orecv.at[x], xpeers[d])
        else:
            out[x] = obuf[x]
    for d in (2, 1, 3):
        arrived(("o", d), orecv.at[xs[4 - d]])
        out[xs[4 - d]] = orecv[xs[4 - d]]
    for copy in sent:
        copy.wait_send()


def per_device(tokens, proj_weight, partner_shard, partner_block):
    bf16, f32 = jnp.bfloat16, jnp.float32
    n_sems = 16 * len(CHUNKS) + 9
    out = pl.pallas_call(
        kernel,
        out_shape=jax.ShapeDtypeStruct((4, ROWS, HD), bf16),
        in_specs=[
            pl.BlockSpec(memory_space=pl.ANY),
            pl.BlockSpec(memory_space=pl.ANY),
            pl.BlockSpec(memory_space=pltpu.SMEM),
            pl.BlockSpec(memory_space=pltpu.SMEM),
        ],
        out_specs=pl.BlockSpec(memory_space=pltpu.VMEM),
        scratch_shapes=[
            pltpu.VMEM((ROWS, D), bf16),
            pltpu.VMEM((2, FEAT, 4, 384), bf16),
            pltpu.VMEM((3, D, 512), bf16),
            pltpu.VMEM((3, ROWS // BLK, BLK, 512), bf16),
            pltpu.VMEM((16, ROWS // BLK, BLK, 256), bf16),
            pltpu.VMEM((4, ROWS // BLK, BLK, HD), bf16),
            pltpu.VMEM((4, 2, BLK, HD), bf16),
            pltpu.VMEM((4, 32, HD), bf16),
            pltpu.VMEM((32, 1), f32),
            pltpu.VMEM((32, 1), f32),
            pltpu.VMEM((32, HD), f32),
            pltpu.VMEM((4, ROWS, HD), bf16),
            pltpu.VMEM((4, ROWS, HD), bf16),
            pltpu.SemaphoreType.DMA((2,)),
            pltpu.SemaphoreType.DMA((2 * len(CHUNKS) + 2,)),
            pltpu.SemaphoreType.DMA((n_sems,)),
            pltpu.SemaphoreType.DMA((n_sems,)),
        ],
        compiler_params=pltpu.CompilerParams(
            collective_id=0, has_side_effects=True, vmem_limit_bytes=58 * 2**20
        ),
    )(
        tokens,
        proj_weight,
        jnp.transpose(partner_shard, (2, 0, 1)),
        jnp.transpose(partner_block, (2, 0, 1)),
    )
    return jnp.transpose(out, (1, 0, 2))


def solution(mesh):
    in_specs = (
        P("ctx", "head"),
        P(None, "head", None),
        P("head", None, None),
        P("head", None, None),
    )
    return jax.shard_map(
        per_device, mesh=mesh, in_specs=in_specs, out_specs=P("ctx", "head", None), check_vma=False
    )
```

```python
import functools

import jax
import jax.numpy as jnp
from jax import lax
from jax.experimental import pallas as pl
from jax.experimental.pallas import tpu as pltpu
from jax.sharding import PartitionSpec as P

HD = 128
BLK = 64
ROWS = 1024
D = 4096
FEAT = 512
MESH = pl.DeviceIdType.MESH
CHUNKS = (256, 256, 256, 128, 128)
DIRECT = (len(CHUNKS) - 1,)
ZUP = 2
C2 = 1.4426950408889634 * HD**-0.5


def kernel(
    tokens, weight, part_shard, part_block, out,
    tok, stage, wv, pk, kv, q, gq, gout, gm, gl, gacc, obuf, orecv, ids,
    wsem, lsem, ssem, rsem,
):
    ctx, hd = lax.axis_index("ctx"), lax.axis_index("head")
    zh, x, core = ctx // 8, (ctx // 2) % 4, ctx % 2
    zl, y = hd // 4, hd % 4
    g = zh * 2 + core

    def at_ctx(zh_, x_, core_):
        return (zh_ * 8 + x_ * 2 + core_, hd)

    def at_head(zl_, y_):
        return (ctx, zl_ * 4 + y_)

    up, down, far = (y + 1) % 4, (y + 3) % 4, (y + 2) % 4
    xs = [(x + d) % 4 for d in (0, 1, 2, 3)]
    zpeer = at_head(1 - zl, y)
    ypeer, mpeer = at_head(zl, up), at_head(zl, down)
    cpeer = at_ctx(zh, x, 1 - core)
    hpeer = at_ctx(1 - zh, x, core)
    dpeer = at_ctx(1 - zh, x, 1 - core)
    xpeers = [None] + [at_ctx(zh, xs[d], core) for d in (1, 2, 3)]
    hpeers = [hpeer] + [at_ctx(1 - zh, xs[d], core) for d in (1, 2, 3)]
    gc, gz, gd = zh * 2 + 1 - core, (1 - zh) * 2 + core, (1 - zh) * 2 + 1 - core

    def weight_copy(i):
        return pltpu.make_async_copy(
            weight.at[pl.ds(i * FEAT, FEAT)], stage.at[i % 2], wsem.at[i % 2]
        )

    weight_copy(0).start()
    weight_copy(1).start()

    barrier = pltpu.get_barrier_semaphore()
    everyone = [zpeer, ypeer, mpeer, cpeer, dpeer] + xpeers[1:] + hpeers
    for peer in everyone:
        pl.semaphore_signal(barrier, inc=1, device_id=peer, device_id_type=MESH)
    pl.semaphore_wait(barrier, len(everyone))

    sems = {}
    sent = []
    local = {}

    def sem_of(key):
        return sems.setdefault(key, len(sems))

    def send(key, src, dst, peer):
        i = sem_of(key)
        copy = pltpu.make_async_remote_copy(
            src_ref=src, dst_ref=dst, send_sem=ssem.at[i], recv_sem=rsem.at[i],
            device_id=peer, device_id_type=MESH,
        )
        copy.start()
        sent.append(copy)

    def arrived(key, dst):
        i = sem_of(key)
        pltpu.make_async_remote_copy(
            src_ref=dst, dst_ref=dst, send_sem=ssem.at[i], recv_sem=rsem.at[i],
            device_id=zpeer, device_id_type=MESH,
        ).wait_recv()

    def put(key, src, dst):
        copy = pltpu.make_async_copy(src, dst, lsem.at[len(local)])
        copy.start()
        local[key] = copy

    last = len(CHUNKS) - 1
    starts = [sum(CHUNKS[:c]) for c in range(len(CHUNKS))]

    def rows_of(c):
        return pl.ds(starts[c], CHUNKS[c])

    def blocks_of(c):
        return pl.ds(starts[c] // BLK, CHUNKS[c] // BLK)

    def piece(zl_, y_, c):
        return tok.at[rows_of(c), pl.ds(pl.multiple_of((zl_ * 4 + y_) * FEAT, FEAT), FEAT)]

    def mine(c):
        return tokens.at[rows_of(c), :]

    def give_z(c):
        send(("z", c), mine(c), piece(zl, y, c), zpeer)

    def give_y(c):
        send(("yu", c), mine(c), piece(zl, y, c), ypeer)
        send(("yd", c), mine(c), piece(zl, y, c), mpeer)

    def pass_z(c):
        arrived(("z", c), piece(1 - zl, y, c))
        send(("zu", c), piece(1 - zl, y, c), piece(1 - zl, y, c), ypeer)
        send(("zd", c), piece(1 - zl, y, c), piece(1 - zl, y, c), mpeer)

    def pass_y(c):
        arrived(("yu", c), piece(zl, down, c))
        send(("fu", c), piece(zl, down, c), piece(zl, down, c), ypeer)
        arrived(("zd", c), piece(1 - zl, up, c))
        send(("fd", c), piece(1 - zl, up, c), piece(1 - zl, up, c), mpeer)

    def tokens_complete(c):
        arrived(("yd", c), piece(zl, up, c))
        arrived(("zu", c), piece(1 - zl, down, c))
        arrived(("fu", c), piece(zl, far, c))
        arrived(("fd", c), piece(1 - zl, far, c))

    def relayout(i):
        weight_copy(i).wait()
        block = jnp.swapaxes(stage[i % 2], 0, 1)
        rows = pl.ds(i * FEAT, FEAT)
        for h in range(4):
            wv[0, rows, h * HD : (h + 1) * HD] = block[h, :, :HD]
            wv[1 + h // 2, rows, (h % 2) * 256 : (h % 2 + 1) * 256] = block[h, :, HD:]
        if i + 2 < 8:
            weight_copy(i + 2).start()

    def project(c):
        def one(n, carry):
            pk[n, blocks_of(c)] = (
                jnp.dot(tok[rows_of(c), :], wv[n], preferred_element_type=jnp.float32)
                .astype(jnp.bfloat16)
                .reshape(CHUNKS[c] // BLK, BLK, 512)
            )
            return carry

        lax.fori_loop(0, 3, one, 0)

    def kv_part(h, c):
        return pk.at[1 + h // 2, blocks_of(c), :, pl.ds(pl.multiple_of((h % 2) * 256, 256), 256)]

    def q_part(h, c):
        return pk.at[0, blocks_of(c), :, pl.ds(pl.multiple_of(h * HD, HD), HD)]

    def give_x(c):
        for d in (2, 1, 3):
            if c in DIRECT:
                send(("kh", d), kv_part(xs[d], c), kv.at[g * 4 + x, blocks_of(c)], hpeers[d])
            send(("kv", d, c), kv_part(xs[d], c), kv.at[g * 4 + x, blocks_of(c)], xpeers[d])
        if c in DIRECT:
            send(("kh", 0), kv_part(x, c), kv.at[g * 4 + x, blocks_of(c)], hpeer)
        put(("kv", c), kv_part(x, c), kv.at[g * 4 + x, blocks_of(c)])
        for d in (2, 1, 3):
            send(("q", d, c), q_part(xs[d], c), q.at[x, blocks_of(c)], xpeers[d])
        put(("q", c), q_part(x, c), q.at[x, blocks_of(c)])

    def group(k, c):
        return kv.at[pl.ds(k * 4, 4), blocks_of(c)]

    def pass_x(c):
        for d in (1, 2, 3):
            arrived(("kv", d, c), kv.at[g * 4 + xs[4 - d], blocks_of(c)])
        local[("kv", c)].wait()
        if c not in DIRECT:
            send(("kz", c), group(g, c), group(g, c), hpeer)
        send(("kc", c), group(g, c), group(g, c), cpeer)
        for d in (1, 2, 3):
            arrived(("q", d, c), q.at[xs[4 - d], blocks_of(c)])
        local[("q", c)].wait()

    def pass_h(c):
        if c not in DIRECT:
            arrived(("kz", c), group(gz, c))
        else:
            for d in (0, 1, 2, 3):
                arrived(("kh", d), kv.at[gz * 4 + xs[(4 - d) % 4], blocks_of(c)])
        send(("kd", c), group(gz, c), group(gz, c), cpeer)

    def kv_complete(c):
        arrived(("kc", c), group(gc, c))
        arrived(("kd", c), group(gd, c))

    def give_gq():
        lead = q.at[0, pl.ds(0, 2)]
        put("gq", lead, gq.at[g])
        for name, peer in (("gqc", cpeer), ("gqh", hpeer), ("gqd", dpeer)):
            send(name, lead, gq.at[g], peer)

    def take_gq():
        local["gq"].wait()
        arrived("gqc", gq.at[gc])
        arrived("gqh", gq.at[gz])
        arrived("gqd", gq.at[gd])
        gm[...] = jnp.full_like(gm, -jnp.inf)
        gl[...] = jnp.zeros_like(gl)
        gacc[...] = jnp.zeros_like(gacc)

    def lead_keys(c):
        size = CHUNKS[c]
        query = gq[0, g // 2, pl.ds(pl.multiple_of((g % 2) * 32, 32), 32), :]

        def one(k, carry):
            top, total, acc = carry
            block = kv[pl.ds(k * 4, 4), blocks_of(c)].reshape(4 * size, 256)
            s = lax.dot_general(
                query, block[:, :HD], (((1,), (1,)), ((), ())), preferred_element_type=jnp.float32
            )
            higher = jnp.maximum(top, jnp.max(s, axis=1, keepdims=True))
            p = jnp.exp2((s - higher) * C2)
            shrink = jnp.exp2((top - higher) * C2)
            total = total * shrink + jnp.sum(p, axis=1, keepdims=True)
            acc = acc * shrink + jnp.dot(
                p.astype(jnp.bfloat16), block[:, HD:], preferred_element_type=jnp.float32
            )
            return higher, total, acc

        top, total, acc = lax.fori_loop(0, 4, one, (gm[...], gl[...], gacc[...]))
        gm[...], gl[...], gacc[...] = top, total, acc

    def lead_out():
        gout[g] = (gacc[...] / gl[...]).astype(jnp.bfloat16)
        for name, peer in (("goc", cpeer), ("goh", hpeer), ("god", dpeer)):
            send(name, gout.at[g], gout.at[g], peer)

    def slot_of(s):
        return (s & 8) | ((s & 1) << 2) | ((s >> 1) & 3)

    def place_of(b):
        return (slot_of(b >> 4) << 4) | (b & 15)

    def prepare(d):
        def one(r, carry):
            b = ((zh * 8 + xs[d] * 2 + core) << 4) + r
            n = (d * 16 + r) * 6
            for t, k in enumerate(((b + 255) & 255, b, (b + 1) & 255)):
                ids[n + t] = place_of(k)
            for j in range(3):
                ids[n + 3 + j] = (slot_of(part_shard[j, x, b]) << 4) + part_block[j, x, b]
            return carry

        lax.fori_loop(0, 16, one, 0)

    def key_block(i):
        return kv[i >> 4, i & 15]

    def attend(d, r):
        places = [ids[(d * 16 + r) * 6 + t] for t in range(6)]
        places = places[:3] + [0, 1] + places[3:]
        keys = jnp.concatenate([key_block(i) for i in places], axis=0)
        s = lax.dot_general(
            q[xs[d], r], keys[:, :HD], (((1,), (1,)), ((), ())), preferred_element_type=jnp.float32
        )
        p = jnp.exp2((s - jnp.max(s, axis=1, keepdims=True)) * C2).astype(jnp.bfloat16)
        values = jnp.concatenate([keys[:, HD:], jnp.ones((512, HD), jnp.bfloat16)], axis=1)
        o = jnp.dot(p, values, preferred_element_type=jnp.float32)
        obuf[xs[d], r * BLK : (r + 1) * BLK, :] = (o[:, :HD] / o[:, HD:]).astype(jnp.bfloat16)

    give_z(0)
    give_y(0)
    for c in range(1, ZUP):
        give_z(c)
    put("tok", tokens, tok.at[:, pl.ds(pl.multiple_of(hd * FEAT, FEAT), FEAT)])
    for i in range(5):
        relayout(i)
    pass_z(0)
    for i in range(5, 8):
        relayout(i)
    for d in range(4):
        prepare(d)
    local["tok"].wait()
    for c in range(last + 1):
        pass_y(c)
        if ZUP <= c + 2 <= last:
            give_z(c + 2)
        if c + 1 <= last:
            give_y(c + 1)
            pass_z(c + 1)
        if c >= 1:
            pass_x(c - 1)
            if c == 1:
                give_gq()
        if c >= 2:
            pass_h(c - 2)
        tokens_complete(c)
        project(c)
        give_x(c)
        if c >= 2:
            if c == 2:
                kv_complete(0)
                take_gq()
            else:
                kv_complete(c - 2)
            if c < last:
                lead_keys(c - 2)
    pass_h(last - 1)
    pass_x(last)
    kv_complete(last - 1)
    pass_h(last)
    kv_complete(last)
    half = ROWS // 2
    for step, (d, part) in enumerate(((2, 1), (1, 1), (3, 1), (2, 0), (1, 0), (3, 0), (0, 1), (0, 0))):
        if step == 3:
            for c in range(last - 2, last + 1):
                lead_keys(c)
            lead_out()
        for r in range(part * 8, part * 8 + 8):
            attend(d, r)
        rows = pl.ds(part * half, half)
        if step == 3:
            arrived("goc", gout.at[gc])
            arrived("goh", gout.at[gz])
            arrived("god", gout.at[gd])
        if part == 0:
            @pl.when((xs[d] == 0) & (g == 0))
            def _():
                obuf[xs[d], pl.ds(0, 128), :] = gout[...].reshape(128, HD)
        if d:
            send(("o", d, part), obuf.at[xs[d], rows], orecv.at[x, rows], xpeers[d])
        else:
            out[x, rows, :] = obuf[x, rows, :]
    for part in (1, 0):
        rows = pl.ds(part * half, half)
        for d in (2, 1, 3):
            arrived(("o", d, part), orecv.at[xs[4 - d], rows])
            out[xs[4 - d], rows, :] = orecv[xs[4 - d], rows, :]
    for copy in sent:
        copy.wait_send()


def per_device(tokens, proj_weight, partner_shard, partner_block):
    bf16, f32 = jnp.bfloat16, jnp.float32
    n_sems = 16 * len(CHUNKS) + 15
    out = pl.pallas_call(
        kernel,
        out_shape=jax.ShapeDtypeStruct((4, ROWS, HD), bf16),
        in_specs=[
            pl.BlockSpec(memory_space=pl.ANY),
            pl.BlockSpec(memory_space=pl.ANY),
            pl.BlockSpec(memory_space=pltpu.SMEM),
            pl.BlockSpec(memory_space=pltpu.SMEM),
        ],
        out_specs=pl.BlockSpec(memory_space=pltpu.VMEM),
        scratch_shapes=[
            pltpu.VMEM((ROWS, D), bf16),
            pltpu.VMEM((2, FEAT, 4, 384), bf16),
            pltpu.VMEM((3, D, 512), bf16),
            pltpu.VMEM((3, ROWS // BLK, BLK, 512), bf16),
            pltpu.VMEM((16, ROWS // BLK, BLK, 256), bf16),
            pltpu.VMEM((4, ROWS // BLK, BLK, HD), bf16),
            pltpu.VMEM((4, 2, BLK, HD), bf16),
            pltpu.VMEM((4, 32, HD), bf16),
            pltpu.VMEM((32, 1), f32),
            pltpu.VMEM((32, 1), f32),
            pltpu.VMEM((32, HD), f32),
            pltpu.VMEM((4, ROWS, HD), bf16),
            pltpu.VMEM((4, ROWS, HD), bf16),
            pltpu.SMEM((64 * 6,), jnp.int32),
            pltpu.SemaphoreType.DMA((2,)),
            pltpu.SemaphoreType.DMA((2 * len(CHUNKS) + 2,)),
            pltpu.SemaphoreType.DMA((n_sems,)),
            pltpu.SemaphoreType.DMA((n_sems,)),
        ],
        compiler_params=pltpu.CompilerParams(
            collective_id=0, has_side_effects=True, vmem_limit_bytes=58 * 2**20
        ),
    )(
        tokens,
        proj_weight,
        jnp.transpose(partner_shard, (2, 0, 1)),
        jnp.transpose(partner_block, (2, 0, 1)),
    )
    return jnp.transpose(out, (1, 0, 2))


def solution(mesh):
    in_specs = (
        P("ctx", "head"),
        P(None, "head", None),
        P("head", None, None),
        P("head", None, None),
    )
    return jax.shard_map(
        per_device, mesh=mesh, in_specs=in_specs, out_specs=P("ctx", "head", None), check_vma=False
    )
```

```python
import functools

import jax
import jax.numpy as jnp
from jax import lax
from jax.experimental import pallas as pl
from jax.experimental.pallas import tpu as pltpu
from jax.sharding import PartitionSpec as P

HD = 128
BLK = 64
ROWS = 1024
D = 4096
FEAT = 512
MESH = pl.DeviceIdType.MESH
CHUNKS = (256, 256, 256, 128, 128)
DIRECT = (len(CHUNKS) - 1,)
ZUP = 2
PARTS = 4
C2 = 1.4426950408889634 * HD**-0.5


def kernel(
    tokens, weight, part_shard, part_block, out,
    tok, stage, wv, pk, kv, q, gq, gout, gm, gl, gacc, obuf, ids,
    wsem, lsem, ssem, rsem,
):
    ctx, hd = lax.axis_index("ctx"), lax.axis_index("head")
    zh, x, core = ctx // 8, (ctx // 2) % 4, ctx % 2
    zl, y = hd // 4, hd % 4
    g = zh * 2 + core

    def at_ctx(zh_, x_, core_):
        return (zh_ * 8 + x_ * 2 + core_, hd)

    def at_head(zl_, y_):
        return (ctx, zl_ * 4 + y_)

    up, down, far = (y + 1) % 4, (y + 3) % 4, (y + 2) % 4
    xs = [(x + d) % 4 for d in (0, 1, 2, 3)]
    zpeer = at_head(1 - zl, y)
    ypeer, mpeer = at_head(zl, up), at_head(zl, down)
    cpeer = at_ctx(zh, x, 1 - core)
    hpeer = at_ctx(1 - zh, x, core)
    dpeer = at_ctx(1 - zh, x, 1 - core)
    xpeers = [None] + [at_ctx(zh, xs[d], core) for d in (1, 2, 3)]
    hpeers = [hpeer] + [at_ctx(1 - zh, xs[d], core) for d in (1, 2, 3)]
    gc, gz, gd = zh * 2 + 1 - core, (1 - zh) * 2 + core, (1 - zh) * 2 + 1 - core

    def weight_copy(i):
        return pltpu.make_async_copy(
            weight.at[pl.ds(i * FEAT, FEAT)], stage.at[i % 2], wsem.at[i % 2]
        )

    weight_copy(0).start()
    weight_copy(1).start()

    barrier = pltpu.get_barrier_semaphore()
    everyone = [zpeer, ypeer, mpeer, cpeer, dpeer] + xpeers[1:] + hpeers
    for peer in everyone:
        pl.semaphore_signal(barrier, inc=1, device_id=peer, device_id_type=MESH)
    pl.semaphore_wait(barrier, len(everyone))

    sems = {}
    sent = []
    local = {}

    def sem_of(key):
        return sems.setdefault(key, len(sems))

    def send(key, src, dst, peer):
        i = sem_of(key)
        copy = pltpu.make_async_remote_copy(
            src_ref=src, dst_ref=dst, send_sem=ssem.at[i], recv_sem=rsem.at[i],
            device_id=peer, device_id_type=MESH,
        )
        copy.start()
        sent.append(copy)

    def arrived(key, dst):
        i = sem_of(key)
        pltpu.make_async_remote_copy(
            src_ref=dst, dst_ref=dst, send_sem=ssem.at[i], recv_sem=rsem.at[i],
            device_id=zpeer, device_id_type=MESH,
        ).wait_recv()

    def put(key, src, dst):
        copy = pltpu.make_async_copy(src, dst, lsem.at[len(local)])
        copy.start()
        local[key] = copy

    last = len(CHUNKS) - 1
    starts = [sum(CHUNKS[:c]) for c in range(len(CHUNKS))]

    def rows_of(c):
        return pl.ds(starts[c], CHUNKS[c])

    def blocks_of(c):
        return pl.ds(starts[c] // BLK, CHUNKS[c] // BLK)

    def piece(zl_, y_, c):
        return tok.at[rows_of(c), pl.ds(pl.multiple_of((zl_ * 4 + y_) * FEAT, FEAT), FEAT)]

    def mine(c):
        return tokens.at[rows_of(c), :]

    def give_z(c):
        send(("z", c), mine(c), piece(zl, y, c), zpeer)

    def give_y(c):
        send(("yu", c), mine(c), piece(zl, y, c), ypeer)
        send(("yd", c), mine(c), piece(zl, y, c), mpeer)

    def pass_z(c):
        arrived(("z", c), piece(1 - zl, y, c))
        send(("zu", c), piece(1 - zl, y, c), piece(1 - zl, y, c), ypeer)
        send(("zd", c), piece(1 - zl, y, c), piece(1 - zl, y, c), mpeer)

    def pass_y(c):
        arrived(("yu", c), piece(zl, down, c))
        send(("fu", c), piece(zl, down, c), piece(zl, down, c), ypeer)
        arrived(("zd", c), piece(1 - zl, up, c))
        send(("fd", c), piece(1 - zl, up, c), piece(1 - zl, up, c), mpeer)

    def tokens_complete(c):
        arrived(("yd", c), piece(zl, up, c))
        arrived(("zu", c), piece(1 - zl, down, c))
        arrived(("fu", c), piece(zl, far, c))
        arrived(("fd", c), piece(1 - zl, far, c))

    def relayout(i):
        weight_copy(i).wait()
        block = jnp.swapaxes(stage[i % 2], 0, 1)
        rows = pl.ds(i * FEAT, FEAT)
        for h in range(4):
            wv[0, rows, h * HD : (h + 1) * HD] = block[h, :, :HD]
            wv[1 + h // 2, rows, (h % 2) * 256 : (h % 2 + 1) * 256] = block[h, :, HD:]
        if i + 2 < 8:
            weight_copy(i + 2).start()

    def project(c):
        def one(n, carry):
            pk[n, blocks_of(c)] = (
                jnp.dot(tok[rows_of(c), :], wv[n], preferred_element_type=jnp.float32)
                .astype(jnp.bfloat16)
                .reshape(CHUNKS[c] // BLK, BLK, 512)
            )
            return carry

        lax.fori_loop(0, 3, one, 0)

    def kv_part(h, c):
        return pk.at[1 + h // 2, blocks_of(c), :, pl.ds(pl.multiple_of((h % 2) * 256, 256), 256)]

    def q_part(h, c):
        return pk.at[0, blocks_of(c), :, pl.ds(pl.multiple_of(h * HD, HD), HD)]

    def give_x(c):
        for d in (2, 1, 3):
            if c in DIRECT:
                send(("kh", d), kv_part(xs[d], c), kv.at[g * 4 + x, blocks_of(c)], hpeers[d])
            send(("kv", d, c), kv_part(xs[d], c), kv.at[g * 4 + x, blocks_of(c)], xpeers[d])
        if c in DIRECT:
            send(("kh", 0), kv_part(x, c), kv.at[g * 4 + x, blocks_of(c)], hpeer)
        put(("kv", c), kv_part(x, c), kv.at[g * 4 + x, blocks_of(c)])
        for d in (2, 1, 3):
            send(("q", d, c), q_part(xs[d], c), q.at[x, blocks_of(c)], xpeers[d])
        put(("q", c), q_part(x, c), q.at[x, blocks_of(c)])

    def group(k, c):
        return kv.at[pl.ds(k * 4, 4), blocks_of(c)]

    def pass_x(c):
        for d in (1, 2, 3):
            arrived(("kv", d, c), kv.at[g * 4 + xs[4 - d], blocks_of(c)])
        local[("kv", c)].wait()
        if c not in DIRECT:
            send(("kz", c), group(g, c), group(g, c), hpeer)
        send(("kc", c), group(g, c), group(g, c), cpeer)
        for d in (1, 2, 3):
            arrived(("q", d, c), q.at[xs[4 - d], blocks_of(c)])
        local[("q", c)].wait()

    def pass_h(c):
        if c not in DIRECT:
            arrived(("kz", c), group(gz, c))
        else:
            for d in (0, 1, 2, 3):
                arrived(("kh", d), kv.at[gz * 4 + xs[(4 - d) % 4], blocks_of(c)])
        send(("kd", c), group(gz, c), group(gz, c), cpeer)

    def kv_complete(c):
        arrived(("kc", c), group(gc, c))
        arrived(("kd", c), group(gd, c))

    def give_gq():
        lead = q.at[0, pl.ds(0, 2)]
        put("gq", lead, gq.at[g])
        for name, peer in (("gqc", cpeer), ("gqh", hpeer), ("gqd", dpeer)):
            send(name, lead, gq.at[g], peer)

    def take_gq():
        local["gq"].wait()
        arrived("gqc", gq.at[gc])
        arrived("gqh", gq.at[gz])
        arrived("gqd", gq.at[gd])
        gm[...] = jnp.full_like(gm, -jnp.inf)
        gl[...] = jnp.zeros_like(gl)
        gacc[...] = jnp.zeros_like(gacc)

    def lead_keys(c):
        size = 2 * CHUNKS[c]
        query = gq[0].reshape(128, HD)

        def one(k, carry):
            top, total, acc = carry
            block = kv[pl.ds(g * 4 + k * 2, 2), blocks_of(c)].reshape(size, 256)
            s = lax.dot_general(
                query, block[:, :HD], (((1,), (1,)), ((), ())), preferred_element_type=jnp.float32
            )
            higher = jnp.maximum(top, jnp.max(s, axis=1, keepdims=True))
            p = jnp.exp2((s - higher) * C2)
            shrink = jnp.exp2((top - higher) * C2)
            total = total * shrink + jnp.sum(p, axis=1, keepdims=True)
            acc = acc * shrink + jnp.dot(
                p.astype(jnp.bfloat16), block[:, HD:], preferred_element_type=jnp.float32
            )
            return higher, total, acc

        top, total, acc = lax.fori_loop(0, 2, one, (gm[...], gl[...], gacc[...]))
        gm[...], gl[...], gacc[...] = top, total, acc

    def lead_out():
        lane = lax.broadcasted_iota(jnp.int32, (128, HD), 1)
        gout[g, 0] = gacc[...]
        gout[g, 1] = jnp.where(lane < 64, gm[...], gl[...])
        for name, peer in (("goc", cpeer), ("goh", hpeer), ("god", dpeer)):
            send(name, gout.at[g], gout.at[g], peer)

    def slot_of(s):
        return (s & 8) | ((s & 1) << 2) | ((s >> 1) & 3)

    def place_of(b):
        return (slot_of(b >> 4) << 4) | (b & 15)

    def prepare(d):
        def one(r, carry):
            b = ((zh * 8 + xs[d] * 2 + core) << 4) + r
            n = (d * 16 + r) * 6
            for t, k in enumerate(((b + 255) & 255, b, (b + 1) & 255)):
                ids[n + t] = place_of(k)
            for j in range(3):
                ids[n + 3 + j] = (slot_of(part_shard[j, x, b]) << 4) + part_block[j, x, b]
            return carry

        lax.fori_loop(0, 16, one, 0)

    def key_block(i):
        return kv[i >> 4, i & 15]

    def attend(d, r):
        places = [ids[(d * 16 + r) * 6 + t] for t in range(6)]
        places = places[:3] + [0, 1] + places[3:]
        keys = jnp.concatenate([key_block(i) for i in places], axis=0)
        s = lax.dot_general(
            q[xs[d], r], keys[:, :HD], (((1,), (1,)), ((), ())), preferred_element_type=jnp.float32
        )
        p = jnp.exp2((s - jnp.max(s, axis=1, keepdims=True)) * C2).astype(jnp.bfloat16)
        values = jnp.concatenate([keys[:, HD:], jnp.ones((512, HD), jnp.bfloat16)], axis=1)
        o = jnp.dot(p, values, preferred_element_type=jnp.float32)
        obuf[xs[d], r * BLK : (r + 1) * BLK, :] = (o[:, :HD] / o[:, HD:]).astype(jnp.bfloat16)

    def lead_rows(d):
        if d == 2:
            arrived("goc", gout.at[gc])
            arrived("goh", gout.at[gz])
            arrived("god", gout.at[gd])

        @pl.when((xs[d] == 0) & (g == 0))
        def _():
            tops = [gout[k, 1, :, 0:1] for k in range(4)]
            totals = [gout[k, 1, :, 64:65] for k in range(4)]
            top = functools.reduce(jnp.maximum, tops)
            shrink = [jnp.exp2((t - top) * C2) for t in tops]
            total = sum(t * f for t, f in zip(totals, shrink))
            acc = sum(gout[k, 0] * shrink[k] for k in range(4))
            obuf[xs[d], pl.ds(0, 128), :] = (acc / total).astype(jnp.bfloat16)

    give_z(0)
    give_y(0)
    for c in range(1, ZUP):
        give_z(c)
    put("tok", tokens, tok.at[:, pl.ds(pl.multiple_of(hd * FEAT, FEAT), FEAT)])
    for i in range(4):
        relayout(i)
    pass_z(0)
    for i in range(4, 6):
        relayout(i)
    pass_y(0)
    give_z(2)
    give_y(1)
    for i in range(6, 8):
        relayout(i)
    pass_z(1)
    for d in range(4):
        prepare(d)
    local["tok"].wait()
    for c in range(last + 1):
        if c:
            pass_y(c)
            if c + 2 <= last:
                give_z(c + 2)
            if c + 1 <= last:
                give_y(c + 1)
                pass_z(c + 1)
        if c >= 1:
            pass_x(c - 1)
            if c == 1:
                give_gq()
        if c >= 2:
            pass_h(c - 2)
            if c == 2:
                take_gq()
            lead_keys(c - 2)
        tokens_complete(c)
        project(c)
        give_x(c)
    pass_h(last - 1)
    lead_keys(last - 1)
    pass_x(last)
    lead_keys(last)
    pass_h(last)
    for c in range(last + 1):
        kv_complete(c)
    lead_out()
    size = ROWS // PARTS
    for part in range(PARTS - 1, -1, -1):
        rows = pl.ds(part * size, size)
        for d in (2, 1, 3):
            for r in range(part * size // BLK, (part + 1) * size // BLK):
                attend(d, r)
            if part == 0:
                lead_rows(d)
            send(("o", d, part), obuf.at[xs[d], rows], out.at[x, rows], xpeers[d])
    for r in range(16):
        attend(0, r)
    lead_rows(0)
    put("out", obuf.at[x], out.at[x])
    for part in range(PARTS - 1, -1, -1):
        rows = pl.ds(part * size, size)
        for d in (2, 1, 3):
            arrived(("o", d, part), out.at[xs[4 - d], rows])
    local["out"].wait()
    for copy in sent:
        copy.wait_send()


def per_device(tokens, proj_weight, partner_shard, partner_block):
    bf16, f32 = jnp.bfloat16, jnp.float32
    n_sems = 16 * len(CHUNKS) + 9 + 3 * PARTS
    out = pl.pallas_call(
        kernel,
        out_shape=jax.ShapeDtypeStruct((4, ROWS, HD), bf16),
        in_specs=[
            pl.BlockSpec(memory_space=pl.ANY),
            pl.BlockSpec(memory_space=pl.ANY),
            pl.BlockSpec(memory_space=pltpu.SMEM),
            pl.BlockSpec(memory_space=pltpu.SMEM),
        ],
        out_specs=pl.BlockSpec(memory_space=pl.ANY),
        scratch_shapes=[
            pltpu.VMEM((ROWS, D), bf16),
            pltpu.VMEM((2, FEAT, 4, 384), bf16),
            pltpu.VMEM((3, D, 512), bf16),
            pltpu.VMEM((3, ROWS // BLK, BLK, 512), bf16),
            pltpu.VMEM((16, ROWS // BLK, BLK, 256), bf16),
            pltpu.VMEM((4, ROWS // BLK, BLK, HD), bf16),
            pltpu.VMEM((4, 2, BLK, HD), bf16),
            pltpu.VMEM((4, 2, 128, HD), f32),
            pltpu.VMEM((128, 1), f32),
            pltpu.VMEM((128, 1), f32),
            pltpu.VMEM((128, HD), f32),
            pltpu.VMEM((4, ROWS, HD), bf16),
            pltpu.SMEM((64 * 6,), jnp.int32),
            pltpu.SemaphoreType.DMA((2,)),
            pltpu.SemaphoreType.DMA((2 * len(CHUNKS) + 3,)),
            pltpu.SemaphoreType.DMA((n_sems,)),
            pltpu.SemaphoreType.DMA((n_sems,)),
        ],
        compiler_params=pltpu.CompilerParams(
            collective_id=0, has_side_effects=True, vmem_limit_bytes=58 * 2**20
        ),
    )(
        tokens,
        proj_weight,
        jnp.transpose(partner_shard, (2, 0, 1)),
        jnp.transpose(partner_block, (2, 0, 1)),
    )
    return jnp.transpose(out, (1, 0, 2))


def solution(mesh):
    in_specs = (
        P("ctx", "head"),
        P(None, "head", None),
        P("head", None, None),
        P("head", None, None),
    )
    return jax.shard_map(
        per_device, mesh=mesh, in_specs=in_specs, out_specs=P("ctx", "head", None), check_vma=False
    )
```

```python
import functools

import jax
import jax.numpy as jnp
from jax import lax
from jax.experimental import pallas as pl
from jax.experimental.pallas import tpu as pltpu
from jax.sharding import PartitionSpec as P

HD = 128
BLK = 64
ROWS = 1024
D = 4096
FEAT = 512
MESH = pl.DeviceIdType.MESH
CHUNKS = (128, 256, 256, 256, 128)
DIRECT = (len(CHUNKS) - 1,)
PARTS = 4
C2 = 1.4426950408889634 * HD**-0.5


def kernel(
    tokens, weight, part_shard, part_block, out,
    tok, stage, wv, pk, kv, q, gq, gout, gm, gl, gacc, obuf, ids,
    wsem, lsem, ssem, rsem,
):
    ctx, hd = lax.axis_index("ctx"), lax.axis_index("head")
    zh, x, core = ctx // 8, (ctx // 2) % 4, ctx % 2
    zl, y = hd // 4, hd % 4
    g = zh * 2 + core

    def at_ctx(zh_, x_, core_):
        return (zh_ * 8 + x_ * 2 + core_, hd)

    def at_head(zl_, y_):
        return (ctx, zl_ * 4 + y_)

    up, down, far = (y + 1) % 4, (y + 3) % 4, (y + 2) % 4
    xs = [(x + d) % 4 for d in (0, 1, 2, 3)]
    zpeer = at_head(1 - zl, y)
    ypeer, mpeer = at_head(zl, up), at_head(zl, down)
    cpeer = at_ctx(zh, x, 1 - core)
    hpeer = at_ctx(1 - zh, x, core)
    dpeer = at_ctx(1 - zh, x, 1 - core)
    xpeers = [None] + [at_ctx(zh, xs[d], core) for d in (1, 2, 3)]
    hpeers = [hpeer] + [at_ctx(1 - zh, xs[d], core) for d in (1, 2, 3)]
    gc, gz, gd = zh * 2 + 1 - core, (1 - zh) * 2 + core, (1 - zh) * 2 + 1 - core

    def weight_copy(i):
        return pltpu.make_async_copy(
            weight.at[pl.ds(i * FEAT, FEAT)], stage.at[i % 2], wsem.at[i % 2]
        )

    weight_copy(0).start()
    weight_copy(1).start()

    barrier = pltpu.get_barrier_semaphore()
    everyone = [zpeer, ypeer, mpeer, cpeer, dpeer] + xpeers[1:] + hpeers
    for peer in everyone:
        pl.semaphore_signal(barrier, inc=1, device_id=peer, device_id_type=MESH)
    pl.semaphore_wait(barrier, len(everyone))

    sems = {}
    sent = []
    local = {}

    def sem_of(key):
        return sems.setdefault(key, len(sems))

    def send(key, src, dst, peer):
        i = sem_of(key)
        copy = pltpu.make_async_remote_copy(
            src_ref=src, dst_ref=dst, send_sem=ssem.at[i], recv_sem=rsem.at[i],
            device_id=peer, device_id_type=MESH,
        )
        copy.start()
        sent.append(copy)

    def arrived(key, dst):
        i = sem_of(key)
        pltpu.make_async_remote_copy(
            src_ref=dst, dst_ref=dst, send_sem=ssem.at[i], recv_sem=rsem.at[i],
            device_id=zpeer, device_id_type=MESH,
        ).wait_recv()

    def put(key, src, dst):
        copy = pltpu.make_async_copy(src, dst, lsem.at[len(local)])
        copy.start()
        local[key] = copy

    last = len(CHUNKS) - 1
    starts = [sum(CHUNKS[:c]) for c in range(len(CHUNKS))]

    def rows_of(c):
        return pl.ds(starts[c], CHUNKS[c])

    def blocks_of(c):
        return pl.ds(starts[c] // BLK, CHUNKS[c] // BLK)

    def piece(zl_, y_, c):
        return tok.at[rows_of(c), pl.ds(pl.multiple_of((zl_ * 4 + y_) * FEAT, FEAT), FEAT)]

    def mine(c):
        return tokens.at[rows_of(c), :]

    def give_z(c):
        send(("z", c), mine(c), piece(zl, y, c), zpeer)

    def give_y(c):
        send(("yu", c), mine(c), piece(zl, y, c), ypeer)
        send(("yd", c), mine(c), piece(zl, y, c), mpeer)

    def pass_z(c):
        arrived(("z", c), piece(1 - zl, y, c))
        send(("zu", c), piece(1 - zl, y, c), piece(1 - zl, y, c), ypeer)
        send(("zd", c), piece(1 - zl, y, c), piece(1 - zl, y, c), mpeer)

    def pass_y(c):
        arrived(("yu", c), piece(zl, down, c))
        send(("fu", c), piece(zl, down, c), piece(zl, down, c), ypeer)
        arrived(("zd", c), piece(1 - zl, up, c))
        send(("fd", c), piece(1 - zl, up, c), piece(1 - zl, up, c), mpeer)

    def tokens_complete(c):
        arrived(("yd", c), piece(zl, up, c))
        arrived(("zu", c), piece(1 - zl, down, c))
        arrived(("fu", c), piece(zl, far, c))
        arrived(("fd", c), piece(1 - zl, far, c))

    def relayout(i):
        weight_copy(i).wait()
        block = jnp.swapaxes(stage[i % 2], 0, 1)
        rows = pl.ds(i * FEAT, FEAT)
        for h in range(4):
            wv[0, rows, h * HD : (h + 1) * HD] = block[h, :, :HD]
            wv[1 + h // 2, rows, (h % 2) * 256 : (h % 2 + 1) * 256] = block[h, :, HD:]
        if i + 2 < 8:
            weight_copy(i + 2).start()

    def project(c):
        def one(n, carry):
            pk[n, blocks_of(c)] = (
                jnp.dot(tok[rows_of(c), :], wv[n], preferred_element_type=jnp.float32)
                .astype(jnp.bfloat16)
                .reshape(CHUNKS[c] // BLK, BLK, 512)
            )
            return carry

        lax.fori_loop(0, 3, one, 0)

    def kv_part(h, c):
        return pk.at[1 + h // 2, blocks_of(c), :, pl.ds(pl.multiple_of((h % 2) * 256, 256), 256)]

    def q_part(h, c):
        return pk.at[0, blocks_of(c), :, pl.ds(pl.multiple_of(h * HD, HD), HD)]

    def give_x(c):
        for d in (2, 1, 3):
            if c in DIRECT:
                send(("kh", d), kv_part(xs[d], c), kv.at[g * 4 + x, blocks_of(c)], hpeers[d])
            send(("kv", d, c), kv_part(xs[d], c), kv.at[g * 4 + x, blocks_of(c)], xpeers[d])
        if c in DIRECT:
            send(("kh", 0), kv_part(x, c), kv.at[g * 4 + x, blocks_of(c)], hpeer)
        put(("kv", c), kv_part(x, c), kv.at[g * 4 + x, blocks_of(c)])
        for d in (2, 1, 3):
            send(("q", d, c), q_part(xs[d], c), q.at[x, blocks_of(c)], xpeers[d])
        put(("q", c), q_part(x, c), q.at[x, blocks_of(c)])

    def group(k, c):
        return kv.at[pl.ds(k * 4, 4), blocks_of(c)]

    def pass_x(c):
        for d in (1, 2, 3):
            arrived(("kv", d, c), kv.at[g * 4 + xs[4 - d], blocks_of(c)])
        local[("kv", c)].wait()
        if c not in DIRECT:
            send(("kz", c), group(g, c), group(g, c), hpeer)
        send(("kc", c), group(g, c), group(g, c), cpeer)
        for d in (1, 2, 3):
            arrived(("q", d, c), q.at[xs[4 - d], blocks_of(c)])
        local[("q", c)].wait()

    def pass_h(c):
        if c not in DIRECT:
            arrived(("kz", c), group(gz, c))
        else:
            for d in (0, 1, 2, 3):
                arrived(("kh", d), kv.at[gz * 4 + xs[(4 - d) % 4], blocks_of(c)])
        send(("kd", c), group(gz, c), group(gz, c), cpeer)

    def kv_complete(c):
        arrived(("kc", c), group(gc, c))
        arrived(("kd", c), group(gd, c))

    def give_gq():
        lead = q.at[0, pl.ds(0, 2)]
        put("gq", lead, gq.at[g])
        for name, peer in (("gqc", cpeer), ("gqh", hpeer), ("gqd", dpeer)):
            send(name, lead, gq.at[g], peer)

    def take_gq():
        local["gq"].wait()
        arrived("gqc", gq.at[gc])
        arrived("gqh", gq.at[gz])
        arrived("gqd", gq.at[gd])
        gm[...] = jnp.full_like(gm, -jnp.inf)
        gl[...] = jnp.zeros_like(gl)
        gacc[...] = jnp.zeros_like(gacc)

    def lead_keys(c):
        size = 2 * CHUNKS[c]
        query = gq[0].reshape(128, HD)

        def one(k, carry):
            top, total, acc = carry
            block = kv[pl.ds(g * 4 + k * 2, 2), blocks_of(c)].reshape(size, 256)
            s = lax.dot_general(
                query, block[:, :HD], (((1,), (1,)), ((), ())), preferred_element_type=jnp.float32
            )
            higher = jnp.maximum(top, jnp.max(s, axis=1, keepdims=True))
            p = jnp.exp2((s - higher) * C2)
            shrink = jnp.exp2((top - higher) * C2)
            total = total * shrink + jnp.sum(p, axis=1, keepdims=True)
            acc = acc * shrink + jnp.dot(
                p.astype(jnp.bfloat16), block[:, HD:], preferred_element_type=jnp.float32
            )
            return higher, total, acc

        top, total, acc = lax.fori_loop(0, 2, one, (gm[...], gl[...], gacc[...]))
        gm[...], gl[...], gacc[...] = top, total, acc

    def lead_out():
        lane = lax.broadcasted_iota(jnp.int32, (128, HD), 1)
        gout[g, 0] = gacc[...]
        gout[g, 1] = jnp.where(lane < 64, gm[...], gl[...])
        for name, peer in (("goc", cpeer), ("goh", hpeer), ("god", dpeer)):
            send(name, gout.at[g], gout.at[g], peer)

    def slot_of(s):
        return (s & 8) | ((s & 1) << 2) | ((s >> 1) & 3)

    def place_of(b):
        return (slot_of(b >> 4) << 4) | (b & 15)

    def prepare(d):
        def one(r, carry):
            b = ((zh * 8 + xs[d] * 2 + core) << 4) + r
            n = (d * 16 + r) * 6
            for t, k in enumerate(((b + 255) & 255, b, (b + 1) & 255)):
                ids[n + t] = place_of(k)
            for j in range(3):
                ids[n + 3 + j] = (slot_of(part_shard[j, x, b]) << 4) + part_block[j, x, b]
            return carry

        lax.fori_loop(0, 16, one, 0)

    def key_block(i):
        return kv[i >> 4, i & 15]

    def attend(d, r):
        places = [ids[(d * 16 + r) * 6 + t] for t in range(6)]
        places = places[:3] + [0, 1] + places[3:]
        keys = jnp.concatenate([key_block(i) for i in places], axis=0)
        s = lax.dot_general(
            q[xs[d], r], keys[:, :HD], (((1,), (1,)), ((), ())), preferred_element_type=jnp.float32
        )
        p = jnp.exp2((s - jnp.max(s, axis=1, keepdims=True)) * C2).astype(jnp.bfloat16)
        values = jnp.concatenate([keys[:, HD:], jnp.ones((512, HD), jnp.bfloat16)], axis=1)
        o = jnp.dot(p, values, preferred_element_type=jnp.float32)
        obuf[xs[d], r * BLK : (r + 1) * BLK, :] = (o[:, :HD] / o[:, HD:]).astype(jnp.bfloat16)

    def lead_rows(d):
        if d == 2:
            arrived("goc", gout.at[gc])
            arrived("goh", gout.at[gz])
            arrived("god", gout.at[gd])

        @pl.when((xs[d] == 0) & (g == 0))
        def _():
            tops = [gout[k, 1, :, 0:1] for k in range(4)]
            totals = [gout[k, 1, :, 64:65] for k in range(4)]
            top = functools.reduce(jnp.maximum, tops)
            shrink = [jnp.exp2((t - top) * C2) for t in tops]
            total = sum(t * f for t, f in zip(totals, shrink))
            acc = sum(gout[k, 0] * shrink[k] for k in range(4))
            obuf[xs[d], pl.ds(0, 128), :] = (acc / total).astype(jnp.bfloat16)

    def far_half(k):
        rows = pl.ds(k * CHUNKS[0] // 2, CHUNKS[0] // 2)
        return lambda y_: tok.at[rows, pl.ds(pl.multiple_of((zl * 4 + y_) * FEAT, FEAT), FEAT)]

    def over_z(k, y_):
        send(("b", k), piece(zl, y_, 0), piece(zl, y_, 0), zpeer)

    send(("b", 0), mine(0), piece(zl, y, 0), zpeer)
    give_y(0)
    give_z(1)
    give_y(1)
    put("tok", tokens, tok.at[:, pl.ds(pl.multiple_of(hd * FEAT, FEAT), FEAT)])
    for i in range(3):
        relayout(i)
    arrived(("yu", 0), piece(zl, down, 0))
    send(("fu", 0), far_half(0)(down), far_half(0)(down), ypeer)
    over_z(1, down)
    arrived(("yd", 0), piece(zl, up, 0))
    send(("fd", 0), far_half(1)(up), far_half(1)(up), mpeer)
    over_z(2, up)
    for i in range(3, 6):
        relayout(i)
    pass_z(1)
    arrived(("fu", 0), far_half(0)(far))
    arrived(("fd", 0), far_half(1)(far))
    over_z(3, far)
    give_z(2)
    for i in range(6, 8):
        relayout(i)
    for d in range(4):
        prepare(d)
    local["tok"].wait()
    pass_y(1)
    give_y(2)
    for k, y_ in enumerate((y, down, up, far)):
        arrived(("b", k), piece(1 - zl, y_, 0))
    project(0)
    give_x(0)
    pass_z(2)
    give_z(3)
    for c in range(1, last + 1):
        if c >= 2:
            pass_y(c)
            if c + 2 <= last:
                give_z(c + 2)
            if c + 1 <= last:
                give_y(c + 1)
                pass_z(c + 1)
        pass_x(c - 1)
        if c == 1:
            give_gq()
        if c >= 2:
            pass_h(c - 2)
            if c == 2:
                take_gq()
            lead_keys(c - 2)
        tokens_complete(c)
        project(c)
        give_x(c)
    pass_h(last - 1)
    lead_keys(last - 1)
    pass_x(last)
    lead_keys(last)
    pass_h(last)
    for c in range(last + 1):
        kv_complete(c)
    lead_out()
    size = ROWS // PARTS
    for part in range(PARTS - 1, -1, -1):
        rows = pl.ds(part * size, size)
        for d in (2, 1, 3):
            for r in range(part * size // BLK, (part + 1) * size // BLK):
                attend(d, r)
            if part == 0:
                lead_rows(d)
            send(("o", d, part), obuf.at[xs[d], rows], out.at[x, rows], xpeers[d])
    for r in range(16):
        attend(0, r)
    lead_rows(0)
    put("out", obuf.at[x], out.at[x])
    for part in range(PARTS - 1, -1, -1):
        rows = pl.ds(part * size, size)
        for d in (2, 1, 3):
            arrived(("o", d, part), out.at[xs[4 - d], rows])
    local["out"].wait()
    for copy in sent:
        copy.wait_send()


def per_device(tokens, proj_weight, partner_shard, partner_block):
    bf16, f32 = jnp.bfloat16, jnp.float32
    n_sems = 16 * len(CHUNKS) + 10 + 3 * PARTS
    out = pl.pallas_call(
        kernel,
        out_shape=jax.ShapeDtypeStruct((4, ROWS, HD), bf16),
        in_specs=[
            pl.BlockSpec(memory_space=pl.ANY),
            pl.BlockSpec(memory_space=pl.ANY),
            pl.BlockSpec(memory_space=pltpu.SMEM),
            pl.BlockSpec(memory_space=pltpu.SMEM),
        ],
        out_specs=pl.BlockSpec(memory_space=pl.ANY),
        scratch_shapes=[
            pltpu.VMEM((ROWS, D), bf16),
            pltpu.VMEM((2, FEAT, 4, 384), bf16),
            pltpu.VMEM((3, D, 512), bf16),
            pltpu.VMEM((3, ROWS // BLK, BLK, 512), bf16),
            pltpu.VMEM((16, ROWS // BLK, BLK, 256), bf16),
            pltpu.VMEM((4, ROWS // BLK, BLK, HD), bf16),
            pltpu.VMEM((4, 2, BLK, HD), bf16),
            pltpu.VMEM((4, 2, 128, HD), f32),
            pltpu.VMEM((128, 1), f32),
            pltpu.VMEM((128, 1), f32),
            pltpu.VMEM((128, HD), f32),
            pltpu.VMEM((4, ROWS, HD), bf16),
            pltpu.SMEM((64 * 6,), jnp.int32),
            pltpu.SemaphoreType.DMA((2,)),
            pltpu.SemaphoreType.DMA((2 * len(CHUNKS) + 3,)),
            pltpu.SemaphoreType.DMA((n_sems,)),
            pltpu.SemaphoreType.DMA((n_sems,)),
        ],
        compiler_params=pltpu.CompilerParams(
            collective_id=0, has_side_effects=True, vmem_limit_bytes=58 * 2**20
        ),
    )(
        tokens,
        proj_weight,
        jnp.transpose(partner_shard, (2, 0, 1)),
        jnp.transpose(partner_block, (2, 0, 1)),
    )
    return jnp.transpose(out, (1, 0, 2))


def solution(mesh):
    in_specs = (
        P("ctx", "head"),
        P(None, "head", None),
        P("head", None, None),
        P("head", None, None),
    )
    return jax.shard_map(
        per_device, mesh=mesh, in_specs=in_specs, out_specs=P("ctx", "head", None), check_vma=False
    )
```

```python
import functools

import jax
import jax.numpy as jnp
from jax import lax
from jax.experimental import pallas as pl
from jax.experimental.pallas import tpu as pltpu
from jax.sharding import PartitionSpec as P

HD = 128
BLK = 64
ROWS = 1024
D = 4096
FEAT = 512
MESH = pl.DeviceIdType.MESH
CHUNKS = (128, 320, 256, 192, 128)
DIRECT = (len(CHUNKS) - 1,)
PARTS = 4
C2 = 1.4426950408889634 * HD**-0.5


def kernel(
    tokens, weight, part_shard, part_block, out,
    tok, stage, wv, pk, kv, q, gq, gout, gm, gl, gacc, obuf, ids,
    wsem, lsem, ssem, rsem,
):
    ctx, hd = lax.axis_index("ctx"), lax.axis_index("head")
    zh, x, core = ctx // 8, (ctx // 2) % 4, ctx % 2
    zl, y = hd // 4, hd % 4
    g = zh * 2 + core

    def at_ctx(zh_, x_, core_):
        return (zh_ * 8 + x_ * 2 + core_, hd)

    def at_head(zl_, y_):
        return (ctx, zl_ * 4 + y_)

    up, down, far = (y + 1) % 4, (y + 3) % 4, (y + 2) % 4
    xs = [(x + d) % 4 for d in (0, 1, 2, 3)]
    zpeer = at_head(1 - zl, y)
    ypeer, mpeer = at_head(zl, up), at_head(zl, down)
    cpeer = at_ctx(zh, x, 1 - core)
    hpeer = at_ctx(1 - zh, x, core)
    dpeer = at_ctx(1 - zh, x, 1 - core)
    xpeers = [None] + [at_ctx(zh, xs[d], core) for d in (1, 2, 3)]
    hpeers = [hpeer] + [at_ctx(1 - zh, xs[d], core) for d in (1, 2, 3)]
    gc, gz, gd = zh * 2 + 1 - core, (1 - zh) * 2 + core, (1 - zh) * 2 + 1 - core

    def weight_copy(i):
        return pltpu.make_async_copy(
            weight.at[pl.ds(i * FEAT, FEAT)], stage.at[i % 2], wsem.at[i % 2]
        )

    weight_copy(0).start()
    weight_copy(1).start()

    barrier = pltpu.get_barrier_semaphore()
    everyone = [zpeer, ypeer, mpeer, cpeer, dpeer] + xpeers[1:] + hpeers
    for peer in everyone:
        pl.semaphore_signal(barrier, inc=1, device_id=peer, device_id_type=MESH)
    pl.semaphore_wait(barrier, len(everyone))

    sems = {}
    sent = []
    local = {}

    def sem_of(key):
        return sems.setdefault(key, len(sems))

    def send(key, src, dst, peer):
        i = sem_of(key)
        copy = pltpu.make_async_remote_copy(
            src_ref=src, dst_ref=dst, send_sem=ssem.at[i], recv_sem=rsem.at[i],
            device_id=peer, device_id_type=MESH,
        )
        copy.start()
        sent.append(copy)

    def arrived(key, dst):
        i = sem_of(key)
        pltpu.make_async_remote_copy(
            src_ref=dst, dst_ref=dst, send_sem=ssem.at[i], recv_sem=rsem.at[i],
            device_id=zpeer, device_id_type=MESH,
        ).wait_recv()

    def put(key, src, dst):
        copy = pltpu.make_async_copy(src, dst, lsem.at[len(local)])
        copy.start()
        local[key] = copy

    last = len(CHUNKS) - 1
    starts = [sum(CHUNKS[:c]) for c in range(len(CHUNKS))]

    def rows_of(c):
        return pl.ds(starts[c], CHUNKS[c])

    def blocks_of(c):
        return pl.ds(starts[c] // BLK, CHUNKS[c] // BLK)

    def piece(zl_, y_, c):
        return tok.at[rows_of(c), pl.ds(pl.multiple_of((zl_ * 4 + y_) * FEAT, FEAT), FEAT)]

    def mine(c):
        return tokens.at[rows_of(c), :]

    def give_z(c):
        send(("z", c), mine(c), piece(zl, y, c), zpeer)

    def give_y(c):
        send(("yu", c), mine(c), piece(zl, y, c), ypeer)
        send(("yd", c), mine(c), piece(zl, y, c), mpeer)

    def pass_z(c):
        arrived(("z", c), piece(1 - zl, y, c))
        send(("zu", c), piece(1 - zl, y, c), piece(1 - zl, y, c), ypeer)
        send(("zd", c), piece(1 - zl, y, c), piece(1 - zl, y, c), mpeer)

    def pass_y(c):
        arrived(("yu", c), piece(zl, down, c))
        send(("fu", c), piece(zl, down, c), piece(zl, down, c), ypeer)
        arrived(("zd", c), piece(1 - zl, up, c))
        send(("fd", c), piece(1 - zl, up, c), piece(1 - zl, up, c), mpeer)

    def tokens_complete(c):
        arrived(("yd", c), piece(zl, up, c))
        arrived(("zu", c), piece(1 - zl, down, c))
        arrived(("fu", c), piece(zl, far, c))
        arrived(("fd", c), piece(1 - zl, far, c))

    def relayout(i):
        weight_copy(i).wait()
        block = jnp.swapaxes(stage[i % 2], 0, 1)
        rows = pl.ds(i * FEAT, FEAT)
        for h in range(4):
            wv[0, rows, h * HD : (h + 1) * HD] = block[h, :, :HD]
            wv[1 + h // 2, rows, (h % 2) * 256 : (h % 2 + 1) * 256] = block[h, :, HD:]
        if i + 2 < 8:
            weight_copy(i + 2).start()

    def project(c):
        def one(n, carry):
            pk[n, blocks_of(c)] = (
                jnp.dot(tok[rows_of(c), :], wv[n], preferred_element_type=jnp.float32)
                .astype(jnp.bfloat16)
                .reshape(CHUNKS[c] // BLK, BLK, 512)
            )
            return carry

        lax.fori_loop(0, 3, one, 0)

    def kv_part(h, c):
        return pk.at[1 + h // 2, blocks_of(c), :, pl.ds(pl.multiple_of((h % 2) * 256, 256), 256)]

    def q_part(h, c):
        return pk.at[0, blocks_of(c), :, pl.ds(pl.multiple_of(h * HD, HD), HD)]

    def give_x(c):
        for d in (2, 1, 3):
            if c in DIRECT:
                send(("kh", d), kv_part(xs[d], c), kv.at[g * 4 + x, blocks_of(c)], hpeers[d])
            send(("kv", d, c), kv_part(xs[d], c), kv.at[g * 4 + x, blocks_of(c)], xpeers[d])
        if c in DIRECT:
            send(("kh", 0), kv_part(x, c), kv.at[g * 4 + x, blocks_of(c)], hpeer)
        put(("kv", c), kv_part(x, c), kv.at[g * 4 + x, blocks_of(c)])
        for d in (2, 1, 3):
            send(("q", d, c), q_part(xs[d], c), q.at[x, blocks_of(c)], xpeers[d])
        put(("q", c), q_part(x, c), q.at[x, blocks_of(c)])

    def group(k, c):
        return kv.at[pl.ds(k * 4, 4), blocks_of(c)]

    def pass_x(c):
        for d in (1, 2, 3):
            arrived(("kv", d, c), kv.at[g * 4 + xs[4 - d], blocks_of(c)])
        local[("kv", c)].wait()
        if c not in DIRECT:
            send(("kz", c), group(g, c), group(g, c), hpeer)
        send(("kc", c), group(g, c), group(g, c), cpeer)
        for d in (1, 2, 3):
            arrived(("q", d, c), q.at[xs[4 - d], blocks_of(c)])
        local[("q", c)].wait()

    def pass_h(c):
        if c not in DIRECT:
            arrived(("kz", c), group(gz, c))
        else:
            for d in (0, 1, 2, 3):
                arrived(("kh", d), kv.at[gz * 4 + xs[(4 - d) % 4], blocks_of(c)])
        send(("kd", c), group(gz, c), group(gz, c), cpeer)

    def kv_complete(c):
        arrived(("kc", c), group(gc, c))
        arrived(("kd", c), group(gd, c))

    def give_gq():
        lead = q.at[0, pl.ds(0, 2)]
        put("gq", lead, gq.at[g])
        for name, peer in (("gqc", cpeer), ("gqh", hpeer), ("gqd", dpeer)):
            send(name, lead, gq.at[g], peer)

    def take_gq():
        local["gq"].wait()
        arrived("gqc", gq.at[gc])
        arrived("gqh", gq.at[gz])
        arrived("gqd", gq.at[gd])
        gm[...] = jnp.full_like(gm, -jnp.inf)
        gl[...] = jnp.zeros_like(gl)
        gacc[...] = jnp.zeros_like(gacc)

    def lead_keys(c):
        size = 2 * CHUNKS[c]
        query = gq[0].reshape(128, HD)

        def one(k, carry):
            top, total, acc = carry
            block = kv[pl.ds(g * 4 + k * 2, 2), blocks_of(c)].reshape(size, 256)
            s = lax.dot_general(
                query, block[:, :HD], (((1,), (1,)), ((), ())), preferred_element_type=jnp.float32
            )
            higher = jnp.maximum(top, jnp.max(s, axis=1, keepdims=True))
            p = jnp.exp2((s - higher) * C2)
            shrink = jnp.exp2((top - higher) * C2)
            total = total * shrink + jnp.sum(p, axis=1, keepdims=True)
            acc = acc * shrink + jnp.dot(
                p.astype(jnp.bfloat16), block[:, HD:], preferred_element_type=jnp.float32
            )
            return higher, total, acc

        top, total, acc = lax.fori_loop(0, 2, one, (gm[...], gl[...], gacc[...]))
        gm[...], gl[...], gacc[...] = top, total, acc

    def lead_out():
        lane = lax.broadcasted_iota(jnp.int32, (128, HD), 1)
        gout[g, 0] = gacc[...]
        gout[g, 1] = jnp.where(lane < 64, gm[...], gl[...])
        for name, peer in (("goc", cpeer), ("goh", hpeer), ("god", dpeer)):
            send(name, gout.at[g], gout.at[g], peer)

    def slot_of(s):
        return (s & 8) | ((s & 1) << 2) | ((s >> 1) & 3)

    def place_of(b):
        return (slot_of(b >> 4) << 4) | (b & 15)

    def prepare(d):
        def one(r, carry):
            b = ((zh * 8 + xs[d] * 2 + core) << 4) + r
            n = (d * 16 + r) * 6
            for t, k in enumerate(((b + 255) & 255, b, (b + 1) & 255)):
                ids[n + t] = place_of(k)
            for j in range(3):
                ids[n + 3 + j] = (slot_of(part_shard[j, x, b]) << 4) + part_block[j, x, b]
            return carry

        lax.fori_loop(0, 16, one, 0)

    def key_block(i):
        return kv[i >> 4, i & 15]

    def attend(d, r):
        places = [ids[(d * 16 + r) * 6 + t] for t in range(6)]
        places = places[:3] + [0, 1] + places[3:]
        keys = jnp.concatenate([key_block(i) for i in places], axis=0)
        s = lax.dot_general(
            q[xs[d], r], keys[:, :HD], (((1,), (1,)), ((), ())), preferred_element_type=jnp.float32
        )
        p = jnp.exp2((s - jnp.max(s, axis=1, keepdims=True)) * C2).astype(jnp.bfloat16)
        values = jnp.concatenate([keys[:, HD:], jnp.ones((512, HD), jnp.bfloat16)], axis=1)
        o = jnp.dot(p, values, preferred_element_type=jnp.float32)
        obuf[xs[d], r * BLK : (r + 1) * BLK, :] = (o[:, :HD] / o[:, HD:]).astype(jnp.bfloat16)

    def lead_rows(d):
        if d == 2:
            arrived("goc", gout.at[gc])
            arrived("goh", gout.at[gz])
            arrived("god", gout.at[gd])

        @pl.when((xs[d] == 0) & (g == 0))
        def _():
            tops = [gout[k, 1, :, 0:1] for k in range(4)]
            totals = [gout[k, 1, :, 64:65] for k in range(4)]
            top = functools.reduce(jnp.maximum, tops)
            shrink = [jnp.exp2((t - top) * C2) for t in tops]
            total = sum(t * f for t, f in zip(totals, shrink))
            acc = sum(gout[k, 0] * shrink[k] for k in range(4))
            obuf[xs[d], pl.ds(0, 128), :] = (acc / total).astype(jnp.bfloat16)

    def far_half(k):
        rows = pl.ds(k * CHUNKS[0] // 2, CHUNKS[0] // 2)
        return lambda y_: tok.at[rows, pl.ds(pl.multiple_of((zl * 4 + y_) * FEAT, FEAT), FEAT)]

    def over_z(k, y_):
        send(("b", k), piece(zl, y_, 0), piece(zl, y_, 0), zpeer)

    send(("b", 0), mine(0), piece(zl, y, 0), zpeer)
    give_y(0)
    give_z(1)
    give_y(1)
    put("tok", tokens, tok.at[:, pl.ds(pl.multiple_of(hd * FEAT, FEAT), FEAT)])
    for i in range(3):
        relayout(i)
    arrived(("yu", 0), piece(zl, down, 0))
    send(("fu", 0), far_half(0)(down), far_half(0)(down), ypeer)
    over_z(1, down)
    arrived(("yd", 0), piece(zl, up, 0))
    send(("fd", 0), far_half(1)(up), far_half(1)(up), mpeer)
    over_z(2, up)
    for i in range(3, 6):
        relayout(i)
    pass_z(1)
    arrived(("fu", 0), far_half(0)(far))
    arrived(("fd", 0), far_half(1)(far))
    over_z(3, far)
    give_z(2)
    for i in range(6, 8):
        relayout(i)
    for d in range(4):
        prepare(d)
    local["tok"].wait()
    pass_y(1)
    give_y(2)
    for k, y_ in enumerate((y, down, up, far)):
        arrived(("b", k), piece(1 - zl, y_, 0))
    project(0)
    give_x(0)
    pass_z(2)
    give_z(3)
    for c in range(1, last + 1):
        if c >= 2:
            pass_y(c)
            if c + 2 <= last:
                give_z(c + 2)
            if c + 1 <= last:
                give_y(c + 1)
                pass_z(c + 1)
        pass_x(c - 1)
        if c == 1:
            give_gq()
        if c >= 2:
            pass_h(c - 2)
            if c == 2:
                take_gq()
            lead_keys(c - 2)
        tokens_complete(c)
        project(c)
        give_x(c)
    pass_h(last - 1)
    lead_keys(last - 1)
    pass_x(last)
    lead_keys(last)
    pass_h(last)
    for c in range(last + 1):
        kv_complete(c)
    lead_out()
    size = ROWS // PARTS
    for part in range(PARTS - 1, -1, -1):
        rows = pl.ds(part * size, size)
        for d in (2, 1, 3):
            for r in range(part * size // BLK, (part + 1) * size // BLK):
                attend(d, r)
            if part == 0:
                lead_rows(d)
            send(("o", d, part), obuf.at[xs[d], rows], out.at[x, rows], xpeers[d])
    for r in range(16):
        attend(0, r)
    lead_rows(0)
    put("out", obuf.at[x], out.at[x])
    for part in range(PARTS - 1, -1, -1):
        rows = pl.ds(part * size, size)
        for d in (2, 1, 3):
            arrived(("o", d, part), out.at[xs[4 - d], rows])
    local["out"].wait()
    for copy in sent:
        copy.wait_send()


def per_device(tokens, proj_weight, partner_shard, partner_block):
    bf16, f32 = jnp.bfloat16, jnp.float32
    n_sems = 16 * len(CHUNKS) + 10 + 3 * PARTS
    out = pl.pallas_call(
        kernel,
        out_shape=jax.ShapeDtypeStruct((4, ROWS, HD), bf16),
        in_specs=[
            pl.BlockSpec(memory_space=pl.ANY),
            pl.BlockSpec(memory_space=pl.ANY),
            pl.BlockSpec(memory_space=pltpu.SMEM),
            pl.BlockSpec(memory_space=pltpu.SMEM),
        ],
        out_specs=pl.BlockSpec(memory_space=pl.ANY),
        scratch_shapes=[
            pltpu.VMEM((ROWS, D), bf16),
            pltpu.VMEM((2, FEAT, 4, 384), bf16),
            pltpu.VMEM((3, D, 512), bf16),
            pltpu.VMEM((3, ROWS // BLK, BLK, 512), bf16),
            pltpu.VMEM((16, ROWS // BLK, BLK, 256), bf16),
            pltpu.VMEM((4, ROWS // BLK, BLK, HD), bf16),
            pltpu.VMEM((4, 2, BLK, HD), bf16),
            pltpu.VMEM((4, 2, 128, HD), f32),
            pltpu.VMEM((128, 1), f32),
            pltpu.VMEM((128, 1), f32),
            pltpu.VMEM((128, HD), f32),
            pltpu.VMEM((4, ROWS, HD), bf16),
            pltpu.SMEM((64 * 6,), jnp.int32),
            pltpu.SemaphoreType.DMA((2,)),
            pltpu.SemaphoreType.DMA((2 * len(CHUNKS) + 3,)),
            pltpu.SemaphoreType.DMA((n_sems,)),
            pltpu.SemaphoreType.DMA((n_sems,)),
        ],
        compiler_params=pltpu.CompilerParams(
            collective_id=0, has_side_effects=True, vmem_limit_bytes=58 * 2**20
        ),
    )(
        tokens,
        proj_weight,
        jnp.transpose(partner_shard, (2, 0, 1)),
        jnp.transpose(partner_block, (2, 0, 1)),
    )
    return jnp.transpose(out, (1, 0, 2))


def solution(mesh):
    in_specs = (
        P("ctx", "head"),
        P(None, "head", None),
        P("head", None, None),
        P("head", None, None),
    )
    return jax.shard_map(
        per_device, mesh=mesh, in_specs=in_specs, out_specs=P("ctx", "head", None), check_vma=False
    )
```

```python
import functools

import jax
import jax.numpy as jnp
from jax import lax
from jax.experimental import pallas as pl
from jax.experimental.pallas import tpu as pltpu
from jax.sharding import PartitionSpec as P

HD = 128
BLK = 64
ROWS = 1024
D = 4096
FEAT = 512
MESH = pl.DeviceIdType.MESH
CHUNKS = (128, 320, 256, 192, 128)
DIRECT = (len(CHUNKS) - 1,)
PARTS = 4
C2 = 1.4426950408889634 * HD**-0.5


def kernel(
    tokens, weight, part_shard, part_block, out,
    tok, stage, wv, pk, kv, q, gq, gout, gm, gl, gacc, obuf, ids,
    wsem, lsem, ssem, rsem,
):
    ctx, hd = lax.axis_index("ctx"), lax.axis_index("head")
    zh, x, core = ctx // 8, (ctx // 2) % 4, ctx % 2
    zl, y = hd // 4, hd % 4
    g = zh * 2 + core

    def at_ctx(zh_, x_, core_):
        return (zh_ * 8 + x_ * 2 + core_, hd)

    def at_head(zl_, y_):
        return (ctx, zl_ * 4 + y_)

    up, down, far = (y + 1) % 4, (y + 3) % 4, (y + 2) % 4
    xs = [(x + d) % 4 for d in (0, 1, 2, 3)]
    zpeer = at_head(1 - zl, y)
    ypeer, mpeer = at_head(zl, up), at_head(zl, down)
    cpeer = at_ctx(zh, x, 1 - core)
    hpeer = at_ctx(1 - zh, x, core)
    dpeer = at_ctx(1 - zh, x, 1 - core)
    xpeers = [None] + [at_ctx(zh, xs[d], core) for d in (1, 2, 3)]
    hpeers = [hpeer] + [at_ctx(1 - zh, xs[d], core) for d in (1, 2, 3)]
    gc, gz, gd = zh * 2 + 1 - core, (1 - zh) * 2 + core, (1 - zh) * 2 + 1 - core

    def weight_copy(i):
        return pltpu.make_async_copy(
            weight.at[pl.ds(i * FEAT, FEAT)], stage.at[i % 2], wsem.at[i % 2]
        )

    weight_copy(0).start()
    weight_copy(1).start()

    barrier = pltpu.get_barrier_semaphore()
    everyone = [zpeer, ypeer, mpeer, cpeer, dpeer] + xpeers[1:] + hpeers
    for peer in everyone:
        pl.semaphore_signal(barrier, inc=1, device_id=peer, device_id_type=MESH)
    pl.semaphore_wait(barrier, len(everyone))

    sems = {}
    sent = []
    local = {}

    def sem_of(key):
        return sems.setdefault(key, len(sems))

    def send(key, src, dst, peer):
        i = sem_of(key)
        copy = pltpu.make_async_remote_copy(
            src_ref=src, dst_ref=dst, send_sem=ssem.at[i], recv_sem=rsem.at[i],
            device_id=peer, device_id_type=MESH,
        )
        copy.start()
        sent.append(copy)

    def arrived(key, dst):
        i = sem_of(key)
        pltpu.make_async_remote_copy(
            src_ref=dst, dst_ref=dst, send_sem=ssem.at[i], recv_sem=rsem.at[i],
            device_id=zpeer, device_id_type=MESH,
        ).wait_recv()

    def put(key, src, dst):
        copy = pltpu.make_async_copy(src, dst, lsem.at[len(local)])
        copy.start()
        local[key] = copy

    last = len(CHUNKS) - 1
    starts = [sum(CHUNKS[:c]) for c in range(len(CHUNKS))]

    def rows_of(c):
        return pl.ds(starts[c], CHUNKS[c])

    def blocks_of(c):
        return pl.ds(starts[c] // BLK, CHUNKS[c] // BLK)

    def piece(zl_, y_, c):
        return tok.at[rows_of(c), pl.ds(pl.multiple_of((zl_ * 4 + y_) * FEAT, FEAT), FEAT)]

    def mine(c):
        return tokens.at[rows_of(c), :]

    def give_z(c):
        send(("z", c), mine(c), piece(zl, y, c), zpeer)

    def give_y(c):
        send(("yu", c), mine(c), piece(zl, y, c), ypeer)
        send(("yd", c), mine(c), piece(zl, y, c), mpeer)

    def pass_z(c):
        arrived(("z", c), piece(1 - zl, y, c))
        send(("zu", c), piece(1 - zl, y, c), piece(1 - zl, y, c), ypeer)
        send(("zd", c), piece(1 - zl, y, c), piece(1 - zl, y, c), mpeer)

    def pass_y(c):
        arrived(("yu", c), piece(zl, down, c))
        send(("fu", c), piece(zl, down, c), piece(zl, down, c), ypeer)
        arrived(("zd", c), piece(1 - zl, up, c))
        send(("fd", c), piece(1 - zl, up, c), piece(1 - zl, up, c), mpeer)

    def tokens_complete(c):
        arrived(("yd", c), piece(zl, up, c))
        arrived(("zu", c), piece(1 - zl, down, c))
        arrived(("fu", c), piece(zl, far, c))
        arrived(("fd", c), piece(1 - zl, far, c))

    def relayout(i):
        weight_copy(i).wait()
        block = jnp.swapaxes(stage[i % 2], 0, 1)
        rows = pl.ds(i * FEAT, FEAT)
        for h in range(4):
            wv[0, rows, h * HD : (h + 1) * HD] = block[h, :, :HD]
            wv[1 + h // 2, rows, (h % 2) * 256 : (h % 2 + 1) * 256] = block[h, :, HD:]
        if i + 2 < 8:
            weight_copy(i + 2).start()

    def project(c):
        def one(n, carry):
            pk[n, blocks_of(c)] = (
                jnp.dot(tok[rows_of(c), :], wv[n], preferred_element_type=jnp.float32)
                .astype(jnp.bfloat16)
                .reshape(CHUNKS[c] // BLK, BLK, 512)
            )
            return carry

        lax.fori_loop(0, 3, one, 0)

    def kv_part(h, c):
        return pk.at[1 + h // 2, blocks_of(c), :, pl.ds(pl.multiple_of((h % 2) * 256, 256), 256)]

    def q_part(h, c):
        return pk.at[0, blocks_of(c), :, pl.ds(pl.multiple_of(h * HD, HD), HD)]

    def give_x(c):
        for d in (2, 1, 3):
            if c in DIRECT:
                send(("kh", d), kv_part(xs[d], c), kv.at[g * 4 + x, blocks_of(c)], hpeers[d])
            send(("kv", d, c), kv_part(xs[d], c), kv.at[g * 4 + x, blocks_of(c)], xpeers[d])
        if c in DIRECT:
            send(("kh", 0), kv_part(x, c), kv.at[g * 4 + x, blocks_of(c)], hpeer)
        put(("kv", c), kv_part(x, c), kv.at[g * 4 + x, blocks_of(c)])
        for d in (2, 1, 3):
            send(("q", d, c), q_part(xs[d], c), q.at[x, blocks_of(c)], xpeers[d])
        put(("q", c), q_part(x, c), q.at[x, blocks_of(c)])

    def group(k, c):
        return kv.at[pl.ds(k * 4, 4), blocks_of(c)]

    def pass_x(c):
        for d in (1, 2, 3):
            arrived(("kv", d, c), kv.at[g * 4 + xs[4 - d], blocks_of(c)])
        local[("kv", c)].wait()
        if c not in DIRECT:
            send(("kz", c), group(g, c), group(g, c), hpeer)
        send(("kc", c), group(g, c), group(g, c), cpeer)
        for d in (1, 2, 3):
            arrived(("q", d, c), q.at[xs[4 - d], blocks_of(c)])
        local[("q", c)].wait()

    def pass_h(c):
        if c not in DIRECT:
            arrived(("kz", c), group(gz, c))
        else:
            for d in (0, 1, 2, 3):
                arrived(("kh", d), kv.at[gz * 4 + xs[(4 - d) % 4], blocks_of(c)])
        send(("kd", c), group(gz, c), group(gz, c), cpeer)

    def kv_complete(c):
        arrived(("kc", c), group(gc, c))
        arrived(("kd", c), group(gd, c))

    def give_gq():
        lead = q.at[0, pl.ds(0, 2)]
        put("gq", lead, gq.at[g])
        for name, peer in (("gqc", cpeer), ("gqh", hpeer), ("gqd", dpeer)):
            send(name, lead, gq.at[g], peer)

    def take_gq():
        local["gq"].wait()
        arrived("gqc", gq.at[gc])
        arrived("gqh", gq.at[gz])
        arrived("gqd", gq.at[gd])
        gm[...] = jnp.full_like(gm, -jnp.inf)
        gl[...] = jnp.zeros_like(gl)
        gacc[...] = jnp.zeros_like(gacc)

    def lead_keys(c):
        size = 2 * CHUNKS[c]
        query = gq[0].reshape(128, HD)

        def one(k, carry):
            top, total, acc = carry
            block = kv[pl.ds(g * 4 + k * 2, 2), blocks_of(c)].reshape(size, 256)
            s = lax.dot_general(
                query, block[:, :HD], (((1,), (1,)), ((), ())), preferred_element_type=jnp.float32
            )
            higher = jnp.maximum(top, jnp.max(s, axis=1, keepdims=True))
            p = jnp.exp2((s - higher) * C2)
            shrink = jnp.exp2((top - higher) * C2)
            total = total * shrink + jnp.sum(p, axis=1, keepdims=True)
            acc = acc * shrink + jnp.dot(
                p.astype(jnp.bfloat16), block[:, HD:], preferred_element_type=jnp.float32
            )
            return higher, total, acc

        top, total, acc = lax.fori_loop(0, 2, one, (gm[...], gl[...], gacc[...]))
        gm[...], gl[...], gacc[...] = top, total, acc

    def lead_out():
        lane = lax.broadcasted_iota(jnp.int32, (128, HD), 1)
        gout[g, 0] = gacc[...]
        gout[g, 1] = jnp.where(lane < 64, gm[...], gl[...])
        for name, peer in (("goc", cpeer), ("goh", hpeer), ("god", dpeer)):
            send(name, gout.at[g], gout.at[g], peer)

    def slot_of(s):
        return (s & 8) | ((s & 1) << 2) | ((s >> 1) & 3)

    def place_of(b):
        return (slot_of(b >> 4) << 4) | (b & 15)

    def prepare(d):
        def one(r, carry):
            b = ((zh * 8 + xs[d] * 2 + core) << 4) + r
            n = (d * 16 + r) * 6
            for t, k in enumerate(((b + 255) & 255, b, (b + 1) & 255)):
                ids[n + t] = place_of(k)
            for j in range(3):
                ids[n + 3 + j] = (slot_of(part_shard[j, x, b]) << 4) + part_block[j, x, b]
            return carry

        lax.fori_loop(0, 16, one, 0)

    def key_block(i):
        return kv[i >> 4, i & 15]

    def attend(d, r):
        places = [ids[(d * 16 + r) * 6 + t] for t in range(6)]
        places = places[:3] + [0, 1] + places[3:]
        keys = jnp.concatenate([key_block(i) for i in places], axis=0)
        s = lax.dot_general(
            q[xs[d], r], keys[:, :HD], (((1,), (1,)), ((), ())), preferred_element_type=jnp.float32
        )
        p = jnp.exp2((s - jnp.max(s, axis=1, keepdims=True)) * C2).astype(jnp.bfloat16)
        values = jnp.concatenate([keys[:, HD:], jnp.ones((512, HD), jnp.bfloat16)], axis=1)
        o = jnp.dot(p, values, preferred_element_type=jnp.float32)
        obuf[xs[d], r * BLK : (r + 1) * BLK, :] = (o[:, :HD] / o[:, HD:]).astype(jnp.bfloat16)

    def lead_rows(d):
        if d == 2:
            arrived("goc", gout.at[gc])
            arrived("goh", gout.at[gz])
            arrived("god", gout.at[gd])

        @pl.when((xs[d] == 0) & (g == 0))
        def _():
            tops = [gout[k, 1, :, 0:1] for k in range(4)]
            totals = [gout[k, 1, :, 64:65] for k in range(4)]
            top = functools.reduce(jnp.maximum, tops)
            shrink = [jnp.exp2((t - top) * C2) for t in tops]
            total = sum(t * f for t, f in zip(totals, shrink))
            acc = sum(gout[k, 0] * shrink[k] for k in range(4))
            obuf[xs[d], pl.ds(0, 128), :] = (acc / total).astype(jnp.bfloat16)

    def far_half(k):
        rows = pl.ds(k * CHUNKS[0] // 2, CHUNKS[0] // 2)
        return lambda y_: tok.at[rows, pl.ds(pl.multiple_of((zl * 4 + y_) * FEAT, FEAT), FEAT)]

    def over_z(k, y_):
        send(("b", k), piece(zl, y_, 0), piece(zl, y_, 0), zpeer)

    send(("b", 0), mine(0), piece(zl, y, 0), zpeer)
    give_y(0)
    give_z(1)
    give_y(1)
    put("tok", tokens, tok.at[:, pl.ds(pl.multiple_of(hd * FEAT, FEAT), FEAT)])
    for i in range(3):
        relayout(i)
    arrived(("yu", 0), piece(zl, down, 0))
    send(("fu", 0), far_half(0)(down), far_half(0)(down), ypeer)
    over_z(1, down)
    arrived(("yd", 0), piece(zl, up, 0))
    send(("fd", 0), far_half(1)(up), far_half(1)(up), mpeer)
    over_z(2, up)
    for i in range(3, 6):
        relayout(i)
    pass_z(1)
    arrived(("fu", 0), far_half(0)(far))
    arrived(("fd", 0), far_half(1)(far))
    over_z(3, far)
    give_z(2)
    for i in range(6, 8):
        relayout(i)
    for d in range(4):
        prepare(d)
    local["tok"].wait()
    pass_y(1)
    give_y(2)
    for k, y_ in enumerate((y, down, up, far)):
        arrived(("b", k), piece(1 - zl, y_, 0))
    project(0)
    give_x(0)
    pass_z(2)
    give_z(3)
    for c in range(1, last + 1):
        if c >= 2:
            pass_y(c)
            if c + 2 <= last:
                give_z(c + 2)
            if c + 1 <= last:
                give_y(c + 1)
                pass_z(c + 1)
        pass_x(c - 1)
        if c == 1:
            give_gq()
        if c >= 2:
            pass_h(c - 2)
            if c == 2:
                take_gq()
            lead_keys(c - 2)
        tokens_complete(c)
        project(c)
        give_x(c)
    lead_keys(last - 1)
    pass_h(last - 1)
    pass_x(last)
    lead_keys(last)
    pass_h(last)
    for c in range(last + 1):
        kv_complete(c)
    lead_out()
    size = ROWS // PARTS
    for part in range(PARTS - 1, -1, -1):
        rows = pl.ds(part * size, size)
        for d in (2, 1, 3):
            for r in range(part * size // BLK, (part + 1) * size // BLK):
                attend(d, r)
            if part == 0:
                lead_rows(d)
            send(("o", d, part), obuf.at[xs[d], rows], out.at[x, rows], xpeers[d])
    for r in range(16):
        attend(0, r)
    lead_rows(0)
    put("out", obuf.at[x], out.at[x])
    for part in range(PARTS - 1, -1, -1):
        rows = pl.ds(part * size, size)
        for d in (2, 1, 3):
            arrived(("o", d, part), out.at[xs[4 - d], rows])
    local["out"].wait()
    for copy in sent:
        copy.wait_send()


def per_device(tokens, proj_weight, partner_shard, partner_block):
    bf16, f32 = jnp.bfloat16, jnp.float32
    n_sems = 16 * len(CHUNKS) + 10 + 3 * PARTS
    out = pl.pallas_call(
        kernel,
        out_shape=jax.ShapeDtypeStruct((4, ROWS, HD), bf16),
        in_specs=[
            pl.BlockSpec(memory_space=pl.ANY),
            pl.BlockSpec(memory_space=pl.ANY),
            pl.BlockSpec(memory_space=pltpu.SMEM),
            pl.BlockSpec(memory_space=pltpu.SMEM),
        ],
        out_specs=pl.BlockSpec(memory_space=pl.ANY),
        scratch_shapes=[
            pltpu.VMEM((ROWS, D), bf16),
            pltpu.VMEM((2, FEAT, 4, 384), bf16),
            pltpu.VMEM((3, D, 512), bf16),
            pltpu.VMEM((3, ROWS // BLK, BLK, 512), bf16),
            pltpu.VMEM((16, ROWS // BLK, BLK, 256), bf16),
            pltpu.VMEM((4, ROWS // BLK, BLK, HD), bf16),
            pltpu.VMEM((4, 2, BLK, HD), bf16),
            pltpu.VMEM((4, 2, 128, HD), f32),
            pltpu.VMEM((128, 1), f32),
            pltpu.VMEM((128, 1), f32),
            pltpu.VMEM((128, HD), f32),
            pltpu.VMEM((4, ROWS, HD), bf16),
            pltpu.SMEM((64 * 6,), jnp.int32),
            pltpu.SemaphoreType.DMA((2,)),
            pltpu.SemaphoreType.DMA((2 * len(CHUNKS) + 3,)),
            pltpu.SemaphoreType.DMA((n_sems,)),
            pltpu.SemaphoreType.DMA((n_sems,)),
        ],
        compiler_params=pltpu.CompilerParams(
            collective_id=0, has_side_effects=True, vmem_limit_bytes=58 * 2**20
        ),
    )(
        tokens,
        proj_weight,
        jnp.transpose(partner_shard, (2, 0, 1)),
        jnp.transpose(partner_block, (2, 0, 1)),
    )
    return jnp.transpose(out, (1, 0, 2))


def solution(mesh):
    in_specs = (
        P("ctx", "head"),
        P(None, "head", None),
        P("head", None, None),
        P("head", None, None),
    )
    return jax.shard_map(
        per_device, mesh=mesh, in_specs=in_specs, out_specs=P("ctx", "head", None), check_vma=False
    )
```
